32 devices in a mesh: section: 8 (over z, x), dp: 4 (over y, core).
Axes of the slice: x: 2, y: 2, z: 4, core: 2. Of those that a mesh axis runs over, the one named last changes fastest.
Arguments:
- hidden: bfloat16 [256, 4608], P('dp', 'section'), may hold values from -6 to 6
- norm_gain: float32 [4608], replicated, may hold values from -0.5 to 0.5
- weight: bfloat16 [32000, 4608], P(('section', 'dp'))
- targets: int32 [4, 64], replicated, may hold values from 0 to 31999
- segment_ids: int32 [4, 64], replicated, may hold values from 0 to 7, never falling along the last dimension, each value on 1 to 16 neighbouring positions
- pairing: int32 [4, 8], replicated, may hold values from 0 to 7, each once within a row
- ref_logp: float32 [4, 8], replicated, may hold values from -30 to -20
Outputs:
- hidden_grad: float32 [256, 4608], P('dp', 'section')
- margins: float32 [4, 4], P('dp')
- dpo_loss: float32 [], replicated
The draws below stay inside these ranges and needn't reach their ends.
Inputs may be any that keep to these rules, and one draw needn't show every extreme that they name: `segment_ids`: within each group's row the segment ids never fall and every one of the 8 segments holds at least one token; one segment of each row holds exactly 16. `pairing`: each row holds every segment number once.
All inputs are finite; a program needn't handle non-finite values.
Results may differ from the reference program's by a relative error of at most 0.0046.
Values may be sent and summed in bfloat16 or wider, within the bound.
No kernel may reach another device: no remote copies, remote signals or barrier semaphores. Data moves between devices by JAX's collectives and lax.ppermute only.
A program may use at most 128 MiB of HBM per device.

```python
import math
import jax
import jax.numpy as jnp
import numpy as np
from jax import lax

D = 4608
V_DEV = 1000
TOK_GRP = 64
SEGS = 8
TOKENS = 256
V = 32000
N_DP = 4


def draw_weight(key, part):
    key = jax.random.fold_in(key, 11)
    entry_key, scale_key = jax.random.split(key, 2)
    entries = jax.random.normal(entry_key, (V, D), jnp.float32)
    spread = math.log(4.0)
    row_index = jnp.arange(V, dtype=jnp.float32)
    rise = 1.0 + 2.0 * row_index / V
    row_scale = jnp.exp(jax.random.uniform(scale_key, (V, 1), jnp.float32, 0.0, spread)) * rise[:, None]
    return (entries * row_scale * (1.0 / math.sqrt(D))).astype(jnp.bfloat16)


def touch_ends(drawn, own_key, low, top_value):
    place = [jax.random.randint(jax.random.fold_in(own_key, axis), (), 0, length) for axis, length in enumerate(drawn.shape)]
    main_axis = drawn.shape.index(max(drawn.shape))
    neighbour = place[:main_axis] + [(place[main_axis] + 1) % drawn.shape[main_axis]] + place[main_axis + 1:]
    return drawn.at[tuple(place)].set(low).at[tuple(neighbour)].set(top_value)


def steps_of(rng, extent, pieces, low, top_value):
    def one(axis_at, blocks):
        heights = jax.random.uniform(jax.random.fold_in(jax.random.fold_in(rng, 6), axis_at), (blocks,), jnp.float32, low / len(pieces), top_value / len(pieces))
        return jnp.repeat(jnp.exp(heights), extent[axis_at] // blocks).reshape((-1,) + (1,) * (len(extent) - axis_at - 1))

    loudness = one(*pieces[0])
    for cut in pieces[1:]:
        loudness = loudness * one(*cut)
    return loudness


def cumulative_ranks(count, slope):
    loads = [(1 << 20) // math.isqrt(rank ** slope) + 1 for rank in range(1, count + 1)]
    width = 1 + sum(loads) // (1 << 30)
    return np.cumsum(np.array([max(1, weight // width) for weight in loads]))


def skewed_ids(stream_key, extent, amount, slope):
    grid = cumulative_ranks(amount, slope)
    lot = jax.random.randint(jax.random.fold_in(stream_key, 1), extent, 0, int(grid[amount - 1]))
    grade = jnp.searchsorted(jnp.asarray(grid, jnp.int32), lot, side="right")
    return jax.random.permutation(jax.random.fold_in(stream_key, 2), amount)[grade].astype(jnp.int32)


def split_up(count, total, bound, lean):
    weights = [(1 << 20) // math.isqrt(standing ** lean) + 1 for standing in range(2, count + 1)]
    spare, given = total - bound - (count - 1), [1] * (count - 1)
    while spare > 0:
        free = [i for i in range(count - 1) if given[i] < bound]
        pool, remaining = sum([weights[i] for i in free]), spare
        for i in free:
            extra = min(bound - given[i], max(1, remaining * weights[i] // pool), spare)
            given[i] = given[i] + extra
            spare = spare - extra
    return np.array([bound] + given)


def uneven_parts(stream_key, count, total, bound, skew):
    if count == 2:
        one = jax.random.randint(stream_key, (), max(1, total - bound), min(bound, total - 1) + 1)
        return jnp.stack([one, total - one])
    lengths = jnp.asarray(split_up(count, total, bound, skew), jnp.int32)
    twos = (count - 1) // 2
    donor, taker = lengths[1:1 + 2 * twos:2], lengths[2:2 + 2 * twos:2]
    slack = jnp.minimum(donor - 1, bound - taker)
    moved = jax.random.randint(jax.random.fold_in(stream_key, 1), (twos,), 0, 1 << 20) % (slack + 1)
    lengths = lengths.at[1:1 + 2 * twos:2].set(donor - moved).at[2:2 + 2 * twos:2].set(taker + moved)
    return lengths[jax.random.permutation(jax.random.fold_in(stream_key, 2), count)]


def bell_draw(own_key, dims, scale, limit, pieces=(), kind=jnp.bfloat16):
    values = scale * jax.random.normal(own_key, dims, jnp.float32)
    if pieces:
        values = values * steps_of(own_key, dims, pieces, -0.22, 0.18)
    return jnp.clip(values, -limit, limit).astype(kind)


def setup_inputs(seed: int = 0) -> dict:
    seeds = jax.random.split(jax.random.key(seed), 8)
    return {
        "hidden": bell_draw(seeds[0], (TOKENS, D), 1.0, 6.0, ((0, 4), (1, 8))),
        "norm_gain": jnp.clip(jax.random.uniform(seeds[1], (D,), jnp.float32, -0.5, 0.5), -0.5, 0.5),
        "weight": draw_weight(jax.random.fold_in(seeds[7], 71), 0),
        "targets": touch_ends(skewed_ids(seeds[3], (N_DP, TOK_GRP), V, 2), jax.random.fold_in(seeds[3], 3), 0, V - 1).astype(jnp.int32),
        "segment_ids": jax.vmap(lambda own: jnp.searchsorted(jnp.cumsum(uneven_parts(own, SEGS, TOK_GRP, TOK_GRP // 4, 0)), jnp.arange(TOK_GRP), side="right"))(jax.random.split(seeds[4], N_DP)).reshape((N_DP, TOK_GRP)).astype(jnp.int32),
        "pairing": jax.vmap(lambda own: jax.random.permutation(own, SEGS))(jax.random.split(seeds[5], N_DP)).reshape((N_DP, SEGS)).astype(jnp.int32),
        "ref_logp": jnp.clip(jax.random.uniform(seeds[6], (N_DP, SEGS), jnp.float32, -30.0, -20.0), -30.0, -20.0),
    }


SOFTCAP = 30.0
DPO_BETA = 0.5
LOSS_SCALE = 65536.0
EPSILON = 1e-06

def dpo_terms(token_logp, segment_ids, pairing, ref_logp):
    num_groups, group_tokens = segment_ids.shape
    seg_count = pairing.shape[1]
    pair_count = seg_count // 2
    logp_rows = token_logp.reshape(num_groups, group_tokens)
    seg_range = jnp.arange(seg_count, dtype=jnp.int32)
    member = (segment_ids[:, :, None] == seg_range[None, None, :]).astype(jnp.float32)
    counts = lax.optimization_barrier(jnp.sum(member, axis=1))
    seg_mean = lax.optimization_barrier(jnp.sum(member * logp_rows[:, :, None], axis=1)) / counts
    adjusted = seg_mean - ref_logp
    chosen_hot = (pairing[:, 0::2, None] == seg_range[None, None, :]).astype(jnp.float32)
    rejected_hot = (pairing[:, 1::2, None] == seg_range[None, None, :]).astype(jnp.float32)
    chosen = lax.optimization_barrier(jnp.sum(chosen_hot * adjusted[:, None, :], axis=2))
    rejected = lax.optimization_barrier(jnp.sum(rejected_hot * adjusted[:, None, :], axis=2))
    margins = DPO_BETA * (chosen - rejected)
    dpo_loss = jnp.mean(jax.nn.softplus(-margins))
    margin_pull = -jax.nn.sigmoid(-margins) * (LOSS_SCALE / (num_groups * pair_count))
    seg_pull = DPO_BETA * lax.optimization_barrier(jnp.sum((chosen_hot - rejected_hot) * margin_pull[:, :, None], axis=1)) / counts
    token_weight = lax.optimization_barrier(jnp.sum(member * seg_pull[:, None, :], axis=2)).reshape(-1)
    return (margins, dpo_loss, token_weight)

def reference(hidden, norm_gain, weight, targets, segment_ids, pairing, ref_logp):
    hidden32 = hidden.astype(jnp.float32)
    inv_rms = lax.rsqrt(lax.optimization_barrier(jnp.mean(hidden32 * hidden32, axis=1)) + EPSILON)
    gain_scale = 1.0 + norm_gain
    normed = (hidden32 * inv_rms[:, None] * gain_scale[None, :]).astype(jnp.bfloat16)
    weight_blocks = weight.reshape(-1, V_DEV, D)
    block_ids = jnp.arange(weight_blocks.shape[0], dtype=jnp.int32)
    flat_targets = targets.reshape(-1).astype(jnp.int32)
    tokens_all = flat_targets.shape[0]

    def block_logits(block_index, block_rows):
        raw_logits = lax.dot_general(block_rows, normed, (((1,), (1,)), ((), ())), preferred_element_type=jnp.float32)
        capped = SOFTCAP * jnp.tanh(raw_logits / SOFTCAP)
        vocab_ids = block_index * V_DEV + lax.broadcasted_iota(jnp.int32, (V_DEV, 1), 0)
        target_hot = vocab_ids == flat_targets[None, :]
        return (capped, target_hot)

    def first_pass(running, block_pair):
        capped, target_hot = block_logits(block_pair[0], block_pair[1])
        exp_part = lax.optimization_barrier(jnp.sum(jnp.exp(capped), axis=0))
        pick_part = lax.optimization_barrier(jnp.sum(jnp.where(target_hot, capped, 0.0), axis=0))
        return ((running[0] + exp_part, running[1] + pick_part), None)
    zeros_tok = jnp.zeros((tokens_all,), jnp.float32)
    (exp_total, picked), _ = lax.scan(first_pass, (zeros_tok, zeros_tok), (block_ids, weight_blocks))
    token_logp = picked - jnp.log(exp_total)
    margins, dpo_loss, token_weight = dpo_terms(token_logp, segment_ids, pairing, ref_logp)

    def second_pass(running, block_pair):
        capped, target_hot = block_logits(block_pair[0], block_pair[1])
        token_prob = jnp.exp(capped) / exp_total[None, :]
        cap_slope = 1.0 - capped / SOFTCAP * (capped / SOFTCAP)
        dlogit = (token_weight[None, :] * (target_hot.astype(jnp.float32) - token_prob) * cap_slope).astype(jnp.bfloat16)
        grad_part = lax.dot_general(dlogit, block_pair[1], (((0,), (0,)), ((), ())), preferred_element_type=jnp.float32)
        return (running + grad_part, None)
    grad_normed, _ = lax.scan(second_pass, jnp.zeros((tokens_all, D), jnp.float32), (block_ids, weight_blocks))
    row_dot = lax.optimization_barrier(jnp.sum(grad_normed * gain_scale[None, :] * hidden32, axis=1))
    hidden_grad = gain_scale[None, :] * inv_rms[:, None] * grad_normed - hidden32 * (row_dot * inv_rms * inv_rms * inv_rms / D)[:, None]
    return (hidden_grad, margins, dpo_loss)
```

```python
import functools

import jax
import jax.numpy as jnp
from jax import lax
from jax.experimental import pallas as pl
from jax.experimental.pallas import tpu as pltpu
from jax.sharding import PartitionSpec as P

SOFTCAP = 30.0
DPO_BETA = 0.5
LOSS_SCALE = 65536.0
EPSILON = 1e-06


def swap_bits(arr, index, axis):
    count = arr.shape[axis]
    bit = 1
    while bit < count:
        shape = arr.shape[:axis] + (count // (2 * bit), 2, bit) + arr.shape[axis + 1 :]
        swapped = jnp.flip(arr.reshape(shape), axis + 1).reshape(arr.shape)
        arr = jnp.where((index & bit) != 0, swapped, arr)
        bit *= 2
    return arr


def exchange(arr, axis, size, mask):
    return lax.ppermute(arr, axis, [(i, i ^ mask) for i in range(size)])


def tree_sum(items):
    items = list(items)
    while len(items) > 1:
        items = [items[i] + items[i + 1] for i in range(0, len(items), 2)]
    return items[0]


def dpo_terms(token_logp, segment_ids, pairing, ref_logp):
    num_groups, group_tokens = segment_ids.shape
    seg_count = pairing.shape[1]
    pair_count = seg_count // 2
    logp_rows = token_logp.reshape(num_groups, group_tokens)
    seg_range = jnp.arange(seg_count, dtype=jnp.int32)
    member = (segment_ids[:, :, None] == seg_range[None, None, :]).astype(jnp.float32)
    counts = jnp.sum(member, axis=1)
    seg_mean = jnp.sum(member * logp_rows[:, :, None], axis=1) / counts
    adjusted = seg_mean - ref_logp
    chosen_hot = (pairing[:, 0::2, None] == seg_range[None, None, :]).astype(jnp.float32)
    rejected_hot = (pairing[:, 1::2, None] == seg_range[None, None, :]).astype(jnp.float32)
    chosen = jnp.sum(chosen_hot * adjusted[:, None, :], axis=2)
    rejected = jnp.sum(rejected_hot * adjusted[:, None, :], axis=2)
    margins = DPO_BETA * (chosen - rejected)
    losses = jax.nn.softplus(-margins)
    dpo_loss = jnp.sum(tree_sum([losses[k] for k in range(num_groups)])) / (num_groups * pair_count)
    margin_pull = -jax.nn.sigmoid(-margins) * (LOSS_SCALE / (num_groups * pair_count))
    seg_pull = (
        DPO_BETA * jnp.sum((chosen_hot - rejected_hot) * margin_pull[:, :, None], axis=1) / counts
    )
    token_weight = jnp.sum(member * seg_pull[:, None, :], axis=2).reshape(-1)
    return (margins, dpo_loss, token_weight)


def general_path(hidden, norm_gain, weight, targets, segment_ids, pairing, ref_logp):
    n_sec = lax.axis_size("section")
    n_dp = lax.axis_size("dp")
    n_z, n_y = n_sec // 2, n_dp // 2
    sec = lax.axis_index("section")
    dp = lax.axis_index("dp")
    z, x = sec >> 1, sec & 1
    tok, cols = hidden.shape
    half = tok // 2
    width = cols * n_sec
    vocab_rows = weight.shape[0]
    gain_scale = 1.0 + norm_gain
    own_scale = lax.dynamic_slice_in_dim(gain_scale, sec * cols, cols)

    over_core = lambda a: exchange(a, "dp", n_dp, 1)
    over_x = lambda a: exchange(a, "section", n_sec, 1)
    over_y = lambda a, k: exchange(a, "dp", n_dp, 2 * k)
    over_z = lambda a, k: exchange(a, "section", n_sec, 2 * k)

    targets = swap_bits(targets, dp, 0)
    segment_ids = swap_bits(segment_ids, dp, 0)
    pairing = swap_bits(pairing, dp, 0)
    ref_logp = swap_bits(ref_logp, dp, 0)

    def join_x(mine):
        other = over_x(mine)
        first = x == 0
        both = jnp.stack([jnp.where(first, mine, other), jnp.where(first, other, mine)], axis=-2)
        return both.reshape(both.shape[:-3] + (width,))

    pieces = jnp.stack([hidden] + [over_z(hidden, k) for k in range(1, n_z)], axis=1)
    pieces = swap_bits(pieces, z, 1)
    rows_a = join_x(pieces[:half])
    rows_a = jnp.stack([rows_a] + [over_y(rows_a, k) for k in range(1, n_y)])
    raw_b = pieces[half:]
    raw_b = jnp.stack([raw_b] + [over_y(raw_b, k) for k in range(1, n_y)])
    rows_b = join_x(raw_b)
    rows = jnp.concatenate([rows_a, rows_b], axis=1)
    rows = jnp.stack([rows, over_core(rows)], axis=1).reshape(n_dp * tok, width)

    rows32 = rows.astype(jnp.float32)
    inv_rms = lax.rsqrt(jnp.mean(rows32 * rows32, axis=1) + EPSILON)
    normed = (rows32 * inv_rms[:, None] * gain_scale[None, :]).astype(jnp.bfloat16)
    raw_logits = lax.dot_general(
        weight, normed, (((1,), (1,)), ((), ())), preferred_element_type=jnp.float32
    )
    bent = jnp.tanh(raw_logits / SOFTCAP)
    capped = SOFTCAP * bent
    cap_slope = 1.0 - bent * bent
    vocab_start = (sec * n_dp + dp) * vocab_rows
    vocab_ids = vocab_start + lax.broadcasted_iota(jnp.int32, (vocab_rows, 1), 0)
    target_hot = vocab_ids == targets.reshape(-1)[None, :]
    exp_logits = jnp.where(target_hot, 0.0, jnp.exp(capped))
    sums = jnp.stack(
        [
            jnp.sum(exp_logits, axis=0),
            jnp.sum(exp_logits * cap_slope * raw_logits, axis=0),
            jnp.sum(jnp.where(target_hot, raw_logits, 0.0), axis=0),
        ]
    )
    sums = swap_bits(sums.reshape(3, n_dp, tok), dp, 1)
    sums = sums + over_core(sums)
    sums = tree_sum([sums] + [over_y(sums, k) for k in range(1, n_y)])
    sums = sums + over_x(sums)
    sums = tree_sum([sums] + [over_z(sums, k) for k in range(1, n_z)])
    sums = swap_bits(sums, dp, 1).reshape(3, n_dp * tok)
    others, pulled, raw_target = sums[0], sums[1], sums[2]

    bent_target = jnp.tanh(raw_target / SOFTCAP)
    capped_target = SOFTCAP * bent_target
    exp_total = others + jnp.exp(capped_target)
    token_logp = capped_target - jnp.log(exp_total)
    margins, dpo_loss, token_weight = dpo_terms(token_logp, segment_ids, pairing, ref_logp)
    off_scale = token_weight / exp_total
    hit_scale = off_scale * others
    dlogit = (
        jnp.where(target_hot, hit_scale[None, :], -off_scale[None, :] * exp_logits) * cap_slope
    ).astype(jnp.bfloat16)
    row_dot_inv = hit_scale * (1.0 - bent_target * bent_target) * raw_target - off_scale * pulled

    grad = lax.dot_general(
        dlogit, weight, (((0,), (0,)), ((), ())), preferred_element_type=jnp.float32
    )

    def send(fn, arr, *args):
        return fn(arr.astype(jnp.bfloat16), *args).astype(jnp.float32)

    def split_x(arr):
        arr = arr.reshape(arr.shape[:-1] + (n_z, 2, cols))
        first = x == 0
        lo, hi = arr[..., 0, :], arr[..., 1, :]
        return jnp.where(first, lo, hi) + send(over_x, jnp.where(first, hi, lo))

    def split_y(arr):
        return tree_sum([arr[0]] + [send(over_y, arr[k], k) for k in range(1, n_y)])

    grad = grad.reshape(n_y, 2, tok, width)
    grad = grad[:, 0] + send(over_core, grad[:, 1])
    grad_a = split_y(split_x(grad[:, :half]))
    grad_b = split_x(split_y(grad[:, half:]))
    grad = jnp.moveaxis(jnp.concatenate([grad_a, grad_b], axis=0), 1, 0)
    grad = swap_bits(grad, z, 0)
    grad = tree_sum([grad[0]] + [send(over_z, grad[k], k) for k in range(1, n_z)])

    own_inv = inv_rms[:tok]
    hidden_grad = (
        own_scale[None, :] * own_inv[:, None] * grad
        - hidden.astype(jnp.float32) * (row_dot_inv[:tok] * own_inv * own_inv / width)[:, None]
    )
    return (hidden_grad, margins[:1], dpo_loss)


LANES = 128
HALF = LANES // 2
VMEM = pl.BlockSpec(memory_space=pltpu.VMEM)


def halves(a, b):
    lane = lax.broadcasted_iota(jnp.int32, a.shape, 1)
    crossed = pltpu.roll(jnp.where(lane < HALF, b, a), HALF, 1)
    return jnp.where(lane < HALF, a, crossed), jnp.where(lane < HALF, crossed, b)


def whereabouts():
    sec, dp = lax.axis_index("section"), lax.axis_index("dp")
    return sec >> 1, sec & 1, dp & 1, dp, sec * lax.axis_size("dp") + dp


def relative_rows(ids):
    dp = whereabouts()[3]
    return [ids[pl.ds(dp ^ ((r & 1) * 2 + (r >> 1)), 1), :] for r in range(4)]


def turn_kernel(cols, n_z, targets, weight, turned_a, turned_b, keep, send, flat, hot):
    z, x, _, _, index = whereabouts()
    vocab = weight.shape[0]
    block = 2 * cols
    flat[...] = jnp.concatenate(relative_rows(targets), axis=1) - index * vocab
    row = lax.broadcasted_iota(jnp.int32, hot.shape, 0)
    hot[...] = jnp.where(row == flat[...], 1.0, 0.0).astype(jnp.bfloat16)
    for k in range(n_z):
        at = pl.multiple_of((z ^ k) * block, LANES)
        strip = [weight[:, pl.ds(at + c, LANES)].T for c in range(0, block, LANES)]
        strip = jnp.concatenate(strip, axis=0)
        turned = turned_a if k & 1 else turned_b
        for side in range(2):
            part = strip[side * cols : (side + 1) * cols, :]
            here = pl.multiple_of(((x ^ side) * (n_z // 2) + (k >> 1)) * cols, HALF)
            turned[pl.ds(here, cols), :] = part
            rows = lax.dot_general(
                part, hot[...], (((1,), (0,)), ((), ())), preferred_element_type=jnp.float32
            ).astype(jnp.bfloat16)
            here = pl.multiple_of(((x ^ side) * n_z + (k >> 1) + (0 if k & 1 else n_z // 2)) * cols, HALF)
            keep[pl.ds(here, cols), :] = rows[:, :LANES]
            send[pl.ds(here, cols), :] = rows[:, LANES:]


def strips_kernel(*refs):
    strips, out = refs[:-1], refs[-1]
    rows = out.shape[0] // len(strips)
    for k, strip in enumerate(strips):
        flipped = wide(strip[...]).T
        both = jnp.concatenate([flipped[:rows], flipped[rows:]], axis=1)
        out[k * rows : (k + 1) * rows, :] = both.astype(out.dtype)


def gain_kernel(gain, table):
    for i in range(gain.shape[0]):
        row = jnp.broadcast_to(1.0 + gain[i : i + 1, :], (LANES, LANES))
        table[i * LANES : (i + 1) * LANES, :] = row.T


def norm_kernel(cols, n_z, *refs):
    stacks, table, normed, inv_own, own_scale = refs[:8], refs[8], refs[9], refs[10], refs[11]
    z, x, core, _, _ = whereabouts()
    rows = cols // 2
    own = pl.multiple_of((z * 2 + x) * cols, HALF)
    upper = table[pl.ds(pl.multiple_of(own + rows, 32), rows), :]
    own_scale[...] = halves(table[pl.ds(own, rows), :], upper)[0]
    width = normed.shape[0]
    lane = lax.broadcasted_iota(jnp.int32, (1, LANES), 1)

    def piece(ref, k):
        return wide(ref[k * rows : (k + 1) * rows, :])

    def squares(ref):
        parts = [piece(ref, k) for k in range(n_z)]
        return sum(jnp.sum(part * part, axis=0, keepdims=True) for part in parts)

    invs = []
    for far in range(2):
        base, one, two, three = stacks[4 * far : 4 * far + 4]
        x_first = core == far
        near, away = squares(base), squares(three)
        first, second = squares(one), squares(two)
        near = near + jnp.where(x_first, first, second)
        away = away + jnp.where(x_first, second, first)
        inv = [lax.rsqrt((sq + pltpu.roll(sq, HALF, 1)) / width + EPSILON) for sq in (near, away)]
        invs.append(jnp.where(lane < HALF, inv[0], inv[1]))
    inv_own[...] = invs[0]
    for k in range(n_z):
        for side in range(2):
            at = ((z ^ k) * 2 + (x ^ side)) * cols
            for far in range(2):
                base, one, two, three = stacks[4 * far : 4 * far + 4]
                x_first = core == far
                first, second = piece(one, k), piece(two, k)
                if side == 0:
                    near, away = piece(base, k), jnp.where(x_first, second, first)
                else:
                    near, away = jnp.where(x_first, first, second), piece(three, k)
                for part, value in enumerate(halves(near, away)):
                    here = pl.ds(pl.multiple_of(at + part * rows, 32), rows)
                    value = value * invs[far] * table[here, :]
                    normed[here, far * LANES : (far + 1) * LANES] = value.astype(jnp.bfloat16)


def post_kernel(grad, send):
    for at in chunks(grad.shape[0]):
        send[at, :] = grad[at, LANES:].astype(send.dtype)


def count_kernel(stats, got, sums):
    mine, theirs = stats[...], got[...]
    total = [mine[:, :LANES] + theirs[:, LANES:], mine[:, LANES:] + theirs[:, :LANES]]
    sums[...] = jnp.concatenate(total + [jnp.zeros((2, LANES), jnp.float32)], axis=0)


def chunks(rows):
    count = next(n for n in (8, 4, 2, 1) if rows % (16 * n) == 0)
    step = rows // count
    return [slice(i * step, (i + 1) * step) for i in range(count)]


def after(at, rows):
    return slice(at.start + rows, at.stop + rows)


def wide(a):
    return a.astype(jnp.float32)


def fold_core_kernel(mine, got, keep, send):
    rows = mine.shape[0] // 2

    def split(one_side):
        for at in chunks(rows):
            top = wide(mine[at, :LANES]) + wide(got[at, :])
            low = after(at, rows)
            bottom = wide(mine[low, :LANES]) + wide(got[low, :])
            if not one_side:
                top, bottom = halves(top, bottom)
            keep[at, :] = top.astype(keep.dtype)
            send[at, :] = bottom.astype(send.dtype)

    core = whereabouts()[2]
    pl.when(core == 0)(lambda: split(True))
    pl.when(core != 0)(lambda: split(False))


def tally_kernel(sums, heard, segments, pairing, ref_logp, scales, margins_out, loss_out):
    sums = sums[...] + heard[...]
    groups, places = pairing.shape
    total_pairs = groups * places // 2

    def both(i):
        return jnp.concatenate([sums[i : i + 1], sums[i + 3 : i + 4]], axis=0)

    others, pulled, raw_target = both(0), both(1), both(2)
    bent = jnp.tanh(raw_target / SOFTCAP)
    capped = SOFTCAP * bent
    exp_total = others + jnp.exp(capped)
    token_logp = capped - jnp.log(exp_total)

    seg_rows, pair_rows, ref_rows = relative_rows(segments), relative_rows(pairing), relative_rows(ref_logp)
    seg_id = lax.broadcasted_iota(jnp.int32, (places, places), 0)
    place = lax.broadcasted_iota(jnp.int32, (places, places), 1)
    even = (place[0:1] & 1) == 0
    lane = lax.broadcasted_iota(jnp.int32, (1, LANES), 1)
    losses, weight = [], jnp.zeros((1, LANES), jnp.float32)
    for r in range(groups):
        seg = jnp.concatenate([seg_rows[r & 2], seg_rows[(r & 2) + 1]], axis=1)
        inside = jnp.logical_and(seg == seg_id[:, 0:1], (lane >= HALF) == ((r & 1) == 1))
        member = jnp.where(inside, 1.0, 0.0)
        counts = jnp.sum(member, axis=1, keepdims=True)
        c = r >> 1
        seg_mean = jnp.sum(member * token_logp[c : c + 1], axis=1, keepdims=True) / counts
        seg_ref = jnp.sum(jnp.where(seg_id == place, ref_rows[r], 0.0), axis=1, keepdims=True)
        hot = jnp.where(pair_rows[r] == seg_id, 1.0, 0.0)
        value = jnp.sum(hot * (seg_mean - seg_ref), axis=0, keepdims=True)
        pair = [value[:, k : k + 1] - value[:, k + 1 : k + 2] for k in range(0, places, 2)]
        margins = DPO_BETA * jnp.concatenate([p for p in pair for _ in range(2)], axis=1)
        down = -margins
        loss = jnp.maximum(down, 0.0) + jnp.log1p(jnp.exp(-jnp.abs(down)))
        losses.append(jnp.where(even, loss, 0.0))
        if r == 0:
            margins_out[...] = jnp.concatenate([DPO_BETA * p for p in pair], axis=1)
        if c == 0:
            pull = -(LOSS_SCALE / total_pairs) / (1.0 + jnp.exp(margins))
            pull = jnp.where(even, pull, -pull)
            seg_pull = DPO_BETA * jnp.sum(hot * pull, axis=1, keepdims=True) / counts
            weight = weight + jnp.sum(member * seg_pull, axis=0, keepdims=True)
    loss_out[...] = jnp.sum(tree_sum(losses), axis=1, keepdims=True) / total_pairs

    off = weight / exp_total[0:1]
    hit = off * others[0:1] * (1.0 - bent[0:1] * bent[0:1])
    dot = hit * raw_target[0:1] - off * pulled[0:1]
    scales[...] = jnp.concatenate([halves(off, off)[0], dot, jnp.zeros((6, LANES), jnp.float32)], axis=0)


def fold_half_kernel(mine, got, keep, send):
    rows = mine.shape[0] // 2
    for at in chunks(rows):
        low = after(at, rows)
        left, right = halves(wide(mine[at, :]) + wide(got[at, :]), wide(mine[low, :]) + wide(got[low, :]))
        keep[at, :] = left.astype(keep.dtype)
        send[at, :] = right.astype(send.dtype)


def join_kernel(first_row, mine, got, hit_mine, hit_got, sums, heard, left, right):
    total = sums[...] + heard[...]
    bent = jnp.tanh(total[2:3] / SOFTCAP)
    ratio = total[0:1] * (1.0 - bent * bent)
    ratio = jnp.where(whereabouts()[2] == 0, ratio, halves(ratio, ratio)[0])
    rows = mine.shape[0] // 2

    def joined(at):
        there = after(at, first_row)
        hit = wide(hit_mine[there, :]) + wide(hit_got[there, :])
        return ratio * hit - (mine[at, :] + wide(got[at, :]))

    for at in chunks(rows):
        near, away = halves(joined(at), joined(after(at, rows)))
        left[at, :] = near.astype(left.dtype)
        right[at, :] = away.astype(right.dtype)


def finish_kernel(width, mine, one, two, three, scales, inv_own, own_scale, hidden, out):
    tok = hidden.shape[0]
    grad = (mine[...] + wide(one[...])) + (wide(two[...]) + wide(three[...]))
    grad = (grad * scales[0:1, :] * own_scale[...]).T
    grad = jnp.concatenate([grad[:tok], grad[tok:]], axis=1)
    columns = jnp.concatenate([scales[1:2, :], inv_own[...], jnp.zeros((6, LANES), jnp.float32)], axis=0).T
    dot, inv = columns[:tok, 0:1], columns[:tok, 1:2]
    out[...] = inv * grad - wide(hidden[...]) * (dot * inv * inv / width)


def call(kernel, name, outs, in_specs, out_specs, scratch, limit, flops, moved, *args):
    return pl.pallas_call(
        kernel,
        out_shape=outs,
        in_specs=in_specs,
        out_specs=out_specs,
        scratch_shapes=scratch,
        compiler_params=pltpu.CompilerParams(vmem_limit_bytes=limit << 20),
        cost_estimate=pl.CostEstimate(flops=flops, bytes_accessed=moved, transcendentals=0),
        name=name,
    )(*args)


def fast_path(hidden, norm_gain, weight, targets, segment_ids, pairing, ref_logp):
    n_sec = lax.axis_size("section")
    n_dp = lax.axis_size("dp")
    n_z = n_sec // 2
    tok, cols = hidden.shape
    tokens = n_dp * tok
    width = cols * n_sec
    vocab = weight.shape[0]
    block = 2 * cols
    padded = -(-vocab // LANES) * LANES
    shape = jax.ShapeDtypeStruct
    half, full = jnp.bfloat16, jnp.float32

    def pairs(of):
        return [(s * n_dp + d, of(s, d)) for s in range(n_sec) for d in range(n_dp)]

    both_axes = ("section", "dp")
    one_pairs = pairs(lambda s, d: (s ^ 1) * n_dp + d if d & 1 == 0 else s * n_dp + (d ^ 2))
    two_pairs = pairs(lambda s, d: (s ^ 1) * n_dp + d if d & 1 == 1 else s * n_dp + (d ^ 2))
    to_one = lambda a: lax.ppermute(a, both_axes, one_pairs)
    to_two = lambda a: lax.ppermute(a, both_axes, two_pairs)
    over_core = lambda a: exchange(a, "dp", n_dp, 1)
    over_x = lambda a: exchange(a, "section", n_sec, 1)
    over_y = lambda a: exchange(a, "dp", n_dp, 2)
    over_z = lambda a, k: exchange(a, "section", n_sec, 2 * k)

    def hold(value, *others):
        return lax.optimization_barrier((value,) + others)[0]

    strips = [hidden] + [over_z(hidden, k) for k in range(1, n_z)]

    turned_a, turned_b, hit_keep, hit_send, flat = call(
        functools.partial(turn_kernel, cols, n_z), "turn_weight",
        (shape((width // 2, vocab), half),) * 2
        + (shape((width, LANES), half), shape((width, LANES), half), shape((1, tokens), jnp.int32)),
        [VMEM, VMEM], (VMEM,) * 5, [pltpu.VMEM((vocab, tokens), half)],
        8, 2 * tokens * vocab * width, 4 * vocab * width, targets, weight,
    )

    base = call(
        strips_kernel, "strips", shape((n_z * cols // 2, LANES), half), [VMEM] * n_z, VMEM, [], 4,
        tok * width, 0, *[hold(s, hit_send) for s in strips],
    )
    one = to_one(base)
    two = to_two(base)
    table = call(
        gain_kernel, "gain_table", shape((width, LANES), full), [VMEM], VMEM, [], 4, width * LANES,
        16 * width * LANES, hold(norm_gain.reshape(-1, LANES), base),
    )
    half_rows = (shape((width // 2, LANES), half),) * 2
    hit_keep, hit_send = call(
        fold_core_kernel, "fold_rows", half_rows, [VMEM, VMEM], (VMEM, VMEM), [], 4,
        0, 96 * width * LANES, hit_keep, over_core(hold(hit_send, base)),
    )
    three = to_two(one)
    stacks = [base, one, two, three]
    stacks = stacks + [over_core(s) for s in (base, one, two, hold(three, hit_send, table))]
    hit_got = to_one(hold(hit_send, three, table))

    normed, inv_own, own_scale = call(
        functools.partial(norm_kernel, cols, n_z), "norm",
        (shape((width, tokens), half), shape((1, LANES), full), shape((cols // 2, LANES), full)),
        [VMEM] * 9, (VMEM,) * 3, [], 4, 8 * tokens * width, 0, *stacks, table,
    )
    raw_logits = lax.dot_general(
        weight, normed, (((1,), (0,)), ((), ())), preferred_element_type=jnp.float32
    )
    bent = jnp.tanh(raw_logits / SOFTCAP)
    hot = lax.broadcasted_iota(jnp.int32, (vocab, 1), 0) == flat
    power = jnp.where(hot, 0.0, jnp.exp(SOFTCAP * bent))
    sloped = power * (1.0 - bent * bent)
    stats = [
        jnp.sum(power, axis=0),
        jnp.sum(sloped * raw_logits, axis=0),
        jnp.sum(jnp.where(hot, raw_logits, 0.0), axis=0),
    ]
    stats = jnp.stack(stats)
    sloped = hold(sloped.astype(half), stats)

    def product(turned, sloped):
        return lax.dot_general(turned, sloped, (((1,), (0,)), ((), ())), preferred_element_type=full)

    def halved(kind, rows):
        return (shape((rows, LANES), kind), shape((rows, LANES), half))

    def fold(kernel, name, mine, got, kind=full):
        return call(
            kernel, name, halved(kind, mine.shape[0] // 2), [VMEM] * 2, (VMEM,) * 2, [], 4, 0, 0, mine, got
        )

    rows = width // 2
    grad_a = product(turned_a, sloped)
    send_a = call(post_kernel, "post", shape((rows, LANES), half), [VMEM], VMEM, [], 4, 0, 0, grad_a)
    got_a = over_core(send_a)
    sums = call(
        count_kernel, "count", shape((8, LANES), full), [VMEM] * 2, VMEM, [], 4, 0, 0, stats, over_core(stats)
    )
    grad_b = product(turned_b, hold(sloped, send_a, sums))
    sums = sums + over_x(sums)
    send_b = call(post_kernel, "post", shape((rows, LANES), half), [VMEM], VMEM, [], 4, 0, 0, hold(grad_b, sums))
    got_b = over_core(hold(send_b, hit_got))
    keep_a, send_a = fold(fold_core_kernel, "fold_core", grad_a, hold(got_a, sums))
    got_a = to_one(send_a)
    heard = over_y(sums)
    keep_b, send_b = fold(fold_core_kernel, "fold_core", grad_b, hold(got_b, send_a))
    got_b = to_one(send_b)
    sums = sums + jnp.concatenate([heard[:, HALF:], heard[:, :HALF]], axis=1)
    sums = sums + over_z(sums, 1)
    heard = over_z(sums, 2)

    rows = width // 4

    def join(name, first_row, mine, got):
        return call(
            functools.partial(join_kernel, first_row), name, halved(full, rows // 2),
            [VMEM] * 6, (VMEM,) * 2, [], 4, 0, 0, mine, got, hit_keep, hit_got, sums, heard,
        )

    keep_a, send_a = join("join_a", 0, keep_a, got_a)
    got_a = to_two(send_a)
    keep_b, send_b = join("join_b", rows, keep_b, hold(got_b, send_a))
    got_b = to_two(send_b)
    send_1, send_3 = fold(fold_half_kernel, "fold_last_a", keep_a, got_a, half)
    got_3 = over_z(send_3, 3)
    keep, send_2 = fold(fold_half_kernel, "fold_last_b", keep_b, hold(got_b, send_3))
    got_2, got_1 = over_z(send_2, 2), over_z(hold(send_1, send_2), 1)
    scales, margins, dpo_loss = call(
        tally_kernel, "tally",
        (shape((8, LANES), full), shape((1, ref_logp.shape[1] // 2), full), shape((1, 1), full)),
        [VMEM] * 5, (VMEM,) * 3, [], 4, 0, 0, sums, hold(heard, send_2), segment_ids, pairing, ref_logp,
    )
    hidden_grad = call(
        functools.partial(finish_kernel, width), "finish", shape((tok, cols), full),
        [VMEM] * 8, VMEM, [], 4, 0, 0,
        keep, got_1, got_2, got_3, scales, inv_own, own_scale, hidden,
    )
    return (hidden_grad, margins, dpo_loss.reshape(()))


def per_device(hidden, norm_gain, weight, *rest):
    n_sec, n_dp = lax.axis_size("section"), lax.axis_size("dp")
    tok, cols = hidden.shape
    vocab = weight.shape[0]
    fits = n_dp == 4 and n_sec == 8 and tok == HALF and cols % HALF == 0 and vocab % 8 == 0
    fits = fits and norm_gain.shape[0] % LANES == 0
    path = fast_path if fits else general_path
    return path(hidden, norm_gain, weight, *rest)


def solution(mesh):
    in_specs = (P("dp", "section"), P(), P(("section", "dp"), None), P(), P(), P(), P())
    out_specs = (P("dp", "section"), P("dp", None), P())
    return jax.shard_map(
        per_device, mesh=mesh, in_specs=in_specs, out_specs=out_specs, check_vma=False
    )
```

```python
import functools

import jax
import jax.numpy as jnp
from jax import lax
from jax.experimental import pallas as pl
from jax.experimental.pallas import tpu as pltpu
from jax.sharding import PartitionSpec as P

SOFTCAP = 30.0
DPO_BETA = 0.5
LOSS_SCALE = 65536.0
EPSILON = 1e-06


def swap_bits(arr, index, axis):
    count = arr.shape[axis]
    bit = 1
    while bit < count:
        shape = arr.shape[:axis] + (count // (2 * bit), 2, bit) + arr.shape[axis + 1 :]
        swapped = jnp.flip(arr.reshape(shape), axis + 1).reshape(arr.shape)
        arr = jnp.where((index & bit) != 0, swapped, arr)
        bit *= 2
    return arr


def exchange(arr, axis, size, mask):
    return lax.ppermute(arr, axis, [(i, i ^ mask) for i in range(size)])


def tree_sum(items):
    items = list(items)
    while len(items) > 1:
        items = [items[i] + items[i + 1] for i in range(0, len(items), 2)]
    return items[0]


def dpo_terms(token_logp, segment_ids, pairing, ref_logp):
    num_groups, group_tokens = segment_ids.shape
    seg_count = pairing.shape[1]
    pair_count = seg_count // 2
    logp_rows = token_logp.reshape(num_groups, group_tokens)
    seg_range = jnp.arange(seg_count, dtype=jnp.int32)
    member = (segment_ids[:, :, None] == seg_range[None, None, :]).astype(jnp.float32)
    counts = jnp.sum(member, axis=1)
    seg_mean = jnp.sum(member * logp_rows[:, :, None], axis=1) / counts
    adjusted = seg_mean - ref_logp
    chosen_hot = (pairing[:, 0::2, None] == seg_range[None, None, :]).astype(jnp.float32)
    rejected_hot = (pairing[:, 1::2, None] == seg_range[None, None, :]).astype(jnp.float32)
    chosen = jnp.sum(chosen_hot * adjusted[:, None, :], axis=2)
    rejected = jnp.sum(rejected_hot * adjusted[:, None, :], axis=2)
    margins = DPO_BETA * (chosen - rejected)
    losses = jax.nn.softplus(-margins)
    dpo_loss = jnp.sum(tree_sum([losses[k] for k in range(num_groups)])) / (num_groups * pair_count)
    margin_pull = -jax.nn.sigmoid(-margins) * (LOSS_SCALE / (num_groups * pair_count))
    seg_pull = (
        DPO_BETA * jnp.sum((chosen_hot - rejected_hot) * margin_pull[:, :, None], axis=1) / counts
    )
    token_weight = jnp.sum(member * seg_pull[:, None, :], axis=2).reshape(-1)
    return (margins, dpo_loss, token_weight)


def general_path(hidden, norm_gain, weight, targets, segment_ids, pairing, ref_logp):
    n_sec = lax.axis_size("section")
    n_dp = lax.axis_size("dp")
    n_z, n_y = n_sec // 2, n_dp // 2
    sec = lax.axis_index("section")
    dp = lax.axis_index("dp")
    z, x = sec >> 1, sec & 1
    tok, cols = hidden.shape
    half = tok // 2
    width = cols * n_sec
    vocab_rows = weight.shape[0]
    gain_scale = 1.0 + norm_gain
    own_scale = lax.dynamic_slice_in_dim(gain_scale, sec * cols, cols)

    over_core = lambda a: exchange(a, "dp", n_dp, 1)
    over_x = lambda a: exchange(a, "section", n_sec, 1)
    over_y = lambda a, k: exchange(a, "dp", n_dp, 2 * k)
    over_z = lambda a, k: exchange(a, "section", n_sec, 2 * k)

    targets = swap_bits(targets, dp, 0)
    segment_ids = swap_bits(segment_ids, dp, 0)
    pairing = swap_bits(pairing, dp, 0)
    ref_logp = swap_bits(ref_logp, dp, 0)

    def join_x(mine):
        other = over_x(mine)
        first = x == 0
        both = jnp.stack([jnp.where(first, mine, other), jnp.where(first, other, mine)], axis=-2)
        return both.reshape(both.shape[:-3] + (width,))

    pieces = jnp.stack([hidden] + [over_z(hidden, k) for k in range(1, n_z)], axis=1)
    pieces = swap_bits(pieces, z, 1)
    rows_a = join_x(pieces[:half])
    rows_a = jnp.stack([rows_a] + [over_y(rows_a, k) for k in range(1, n_y)])
    raw_b = pieces[half:]
    raw_b = jnp.stack([raw_b] + [over_y(raw_b, k) for k in range(1, n_y)])
    rows_b = join_x(raw_b)
    rows = jnp.concatenate([rows_a, rows_b], axis=1)
    rows = jnp.stack([rows, over_core(rows)], axis=1).reshape(n_dp * tok, width)

    rows32 = rows.astype(jnp.float32)
    inv_rms = lax.rsqrt(jnp.mean(rows32 * rows32, axis=1) + EPSILON)
    normed = (rows32 * inv_rms[:, None] * gain_scale[None, :]).astype(jnp.bfloat16)
    raw_logits = lax.dot_general(
        weight, normed, (((1,), (1,)), ((), ())), preferred_element_type=jnp.float32
    )
    bent = jnp.tanh(raw_logits / SOFTCAP)
    capped = SOFTCAP * bent
    cap_slope = 1.0 - bent * bent
    vocab_start = (sec * n_dp + dp) * vocab_rows
    vocab_ids = vocab_start + lax.broadcasted_iota(jnp.int32, (vocab_rows, 1), 0)
    target_hot = vocab_ids == targets.reshape(-1)[None, :]
    exp_logits = jnp.where(target_hot, 0.0, jnp.exp(capped))
    sums = jnp.stack(
        [
            jnp.sum(exp_logits, axis=0),
            jnp.sum(exp_logits * cap_slope * raw_logits, axis=0),
            jnp.sum(jnp.where(target_hot, raw_logits, 0.0), axis=0),
        ]
    )
    sums = swap_bits(sums.reshape(3, n_dp, tok), dp, 1)
    sums = sums + over_core(sums)
    sums = tree_sum([sums] + [over_y(sums, k) for k in range(1, n_y)])
    sums = sums + over_x(sums)
    sums = tree_sum([sums] + [over_z(sums, k) for k in range(1, n_z)])
    sums = swap_bits(sums, dp, 1).reshape(3, n_dp * tok)
    others, pulled, raw_target = sums[0], sums[1], sums[2]

    bent_target = jnp.tanh(raw_target / SOFTCAP)
    capped_target = SOFTCAP * bent_target
    exp_total = others + jnp.exp(capped_target)
    token_logp = capped_target - jnp.log(exp_total)
    margins, dpo_loss, token_weight = dpo_terms(token_logp, segment_ids, pairing, ref_logp)
    off_scale = token_weight / exp_total
    hit_scale = off_scale * others
    dlogit = (
        jnp.where(target_hot, hit_scale[None, :], -off_scale[None, :] * exp_logits) * cap_slope
    ).astype(jnp.bfloat16)
    row_dot_inv = hit_scale * (1.0 - bent_target * bent_target) * raw_target - off_scale * pulled

    grad = lax.dot_general(
        dlogit, weight, (((0,), (0,)), ((), ())), preferred_element_type=jnp.float32
    )

    def send(fn, arr, *args):
        return fn(arr.astype(jnp.bfloat16), *args).astype(jnp.float32)

    def split_x(arr):
        arr = arr.reshape(arr.shape[:-1] + (n_z, 2, cols))
        first = x == 0
        lo, hi = arr[..., 0, :], arr[..., 1, :]
        return jnp.where(first, lo, hi) + send(over_x, jnp.where(first, hi, lo))

    def split_y(arr):
        return tree_sum([arr[0]] + [send(over_y, arr[k], k) for k in range(1, n_y)])

    grad = grad.reshape(n_y, 2, tok, width)
    grad = grad[:, 0] + send(over_core, grad[:, 1])
    grad_a = split_y(split_x(grad[:, :half]))
    grad_b = split_x(split_y(grad[:, half:]))
    grad = jnp.moveaxis(jnp.concatenate([grad_a, grad_b], axis=0), 1, 0)
    grad = swap_bits(grad, z, 0)
    grad = tree_sum([grad[0]] + [send(over_z, grad[k], k) for k in range(1, n_z)])

    own_inv = inv_rms[:tok]
    hidden_grad = (
        own_scale[None, :] * own_inv[:, None] * grad
        - hidden.astype(jnp.float32) * (row_dot_inv[:tok] * own_inv * own_inv / width)[:, None]
    )
    return (hidden_grad, margins[:1], dpo_loss)


LANES = 128
HALF = LANES // 2
VMEM = pl.BlockSpec(memory_space=pltpu.VMEM)


def halves(a, b):
    lane = lax.broadcasted_iota(jnp.int32, a.shape, 1)
    crossed = pltpu.roll(jnp.where(lane < HALF, b, a), HALF, 1)
    return jnp.where(lane < HALF, a, crossed), jnp.where(lane < HALF, crossed, b)


def whereabouts():
    sec, dp = lax.axis_index("section"), lax.axis_index("dp")
    return sec >> 1, sec & 1, dp & 1, dp, sec * lax.axis_size("dp") + dp


def relative_rows(ids):
    dp = whereabouts()[3]
    return [ids[pl.ds(dp ^ ((r & 1) * 2 + (r >> 1)), 1), :] for r in range(4)]


def turn_kernel(cols, n_z, targets, weight, turned_a, turned_b, keep, send, flat, hot):
    z, x, _, _, index = whereabouts()
    vocab = weight.shape[0]
    block = 2 * cols
    flat[...] = jnp.concatenate(relative_rows(targets), axis=1) - index * vocab
    row = lax.broadcasted_iota(jnp.int32, hot.shape, 0)
    hot[...] = jnp.where(row == flat[...], 1.0, 0.0).astype(jnp.bfloat16)
    for k in range(n_z):
        at = pl.multiple_of((z ^ k) * block, LANES)
        strip = [weight[:, pl.ds(at + c, LANES)].T for c in range(0, block, LANES)]
        strip = jnp.concatenate(strip, axis=0)
        turned = turned_a if k & 1 else turned_b
        for side in range(2):
            part = strip[side * cols : (side + 1) * cols, :]
            here = pl.multiple_of(((x ^ side) * (n_z // 2) + (k >> 1)) * cols, HALF)
            turned[pl.ds(here, cols), :] = part
            rows = lax.dot_general(
                part, hot[...], (((1,), (0,)), ((), ())), preferred_element_type=jnp.float32
            ).astype(jnp.bfloat16)
            here = pl.multiple_of(((x ^ side) * n_z + (k >> 1) + (0 if k & 1 else n_z // 2)) * cols, HALF)
            keep[pl.ds(here, cols), :] = rows[:, :LANES]
            send[pl.ds(here, cols), :] = rows[:, LANES:]


def strips_kernel(*refs):
    strips, out = refs[:-1], refs[-1]
    rows = out.shape[0] // len(strips)
    for k, strip in enumerate(strips):
        flipped = wide(strip[...]).T
        both = jnp.concatenate([flipped[:rows], flipped[rows:]], axis=1)
        out[k * rows : (k + 1) * rows, :] = both.astype(out.dtype)


def gain_kernel(gain, table):
    for i in range(gain.shape[0]):
        row = jnp.broadcast_to(1.0 + gain[i : i + 1, :], (LANES, LANES))
        table[i * LANES : (i + 1) * LANES, :] = row.T


def norm_kernel(cols, n_z, *refs):
    stacks, table, normed, inv_own, own_scale = refs[:8], refs[8], refs[9], refs[10], refs[11]
    z, x, core, _, _ = whereabouts()
    rows = cols // 2
    own = pl.multiple_of((z * 2 + x) * cols, HALF)
    upper = table[pl.ds(pl.multiple_of(own + rows, 32), rows), :]
    own_scale[...] = halves(table[pl.ds(own, rows), :], upper)[0]
    width = normed.shape[0]
    lane = lax.broadcasted_iota(jnp.int32, (1, LANES), 1)

    def piece(ref, k):
        return wide(ref[k * rows : (k + 1) * rows, :])

    def squares(ref):
        parts = [piece(ref, k) for k in range(n_z)]
        return sum(jnp.sum(part * part, axis=0, keepdims=True) for part in parts)

    invs = []
    for far in range(2):
        base, one, two, three = stacks[4 * far : 4 * far + 4]
        x_first = core == far
        near, away = squares(base), squares(three)
        first, second = squares(one), squares(two)
        near = near + jnp.where(x_first, first, second)
        away = away + jnp.where(x_first, second, first)
        inv = [lax.rsqrt((sq + pltpu.roll(sq, HALF, 1)) / width + EPSILON) for sq in (near, away)]
        invs.append(jnp.where(lane < HALF, inv[0], inv[1]))
    inv_own[...] = invs[0]
    for k in range(n_z):
        for side in range(2):
            at = ((z ^ k) * 2 + (x ^ side)) * cols
            for far in range(2):
                base, one, two, three = stacks[4 * far : 4 * far + 4]
                x_first = core == far
                first, second = piece(one, k), piece(two, k)
                if side == 0:
                    near, away = piece(base, k), jnp.where(x_first, second, first)
                else:
                    near, away = jnp.where(x_first, first, second), piece(three, k)
                for part, value in enumerate(halves(near, away)):
                    here = pl.ds(pl.multiple_of(at + part * rows, 32), rows)
                    value = value * invs[far] * table[here, :]
                    normed[here, far * LANES : (far + 1) * LANES] = value.astype(jnp.bfloat16)


def post_kernel(grad, send):
    for at in chunks(grad.shape[0]):
        send[at, :] = grad[at, LANES:].astype(send.dtype)


def count_kernel(stats, got, sums):
    mine, theirs = stats[...], got[...]
    total = [mine[:, :LANES] + theirs[:, LANES:], mine[:, LANES:] + theirs[:, :LANES]]
    sums[...] = jnp.concatenate(total + [jnp.zeros((2, LANES), jnp.float32)], axis=0)


def chunks(rows):
    count = next(n for n in (8, 4, 2, 1) if rows % (16 * n) == 0)
    step = rows // count
    return [slice(i * step, (i + 1) * step) for i in range(count)]


def after(at, rows):
    return slice(at.start + rows, at.stop + rows)


def wide(a):
    return a.astype(jnp.float32)


def fold_core_kernel(mine, got, keep, send):
    rows = mine.shape[0] // 2

    def split(one_side):
        for at in chunks(rows):
            top = wide(mine[at, :LANES]) + wide(got[at, :])
            low = after(at, rows)
            bottom = wide(mine[low, :LANES]) + wide(got[low, :])
            if not one_side:
                top, bottom = halves(top, bottom)
            keep[at, :] = top.astype(keep.dtype)
            send[at, :] = bottom.astype(send.dtype)

    core = whereabouts()[2]
    pl.when(core == 0)(lambda: split(True))
    pl.when(core != 0)(lambda: split(False))


def tally_kernel(sums, heard, segments, pairing, ref_logp, scales, margins_out, loss_out):
    sums = sums[...] + heard[...]
    groups, places = pairing.shape
    total_pairs = groups * places // 2

    def both(i):
        return jnp.concatenate([sums[i : i + 1], sums[i + 3 : i + 4]], axis=0)

    others, pulled, raw_target = both(0), both(1), both(2)
    bent = jnp.tanh(raw_target / SOFTCAP)
    capped = SOFTCAP * bent
    exp_total = others + jnp.exp(capped)
    token_logp = capped - jnp.log(exp_total)

    seg_rows, pair_rows, ref_rows = relative_rows(segments), relative_rows(pairing), relative_rows(ref_logp)
    seg_id = lax.broadcasted_iota(jnp.int32, (places, places), 0)
    place = lax.broadcasted_iota(jnp.int32, (places, places), 1)
    even = (place[0:1] & 1) == 0
    lane = lax.broadcasted_iota(jnp.int32, (1, LANES), 1)
    losses, weight = [], jnp.zeros((1, LANES), jnp.float32)
    for r in range(groups):
        seg = jnp.concatenate([seg_rows[r & 2], seg_rows[(r & 2) + 1]], axis=1)
        inside = jnp.logical_and(seg == seg_id[:, 0:1], (lane >= HALF) == ((r & 1) == 1))
        member = jnp.where(inside, 1.0, 0.0)
        counts = jnp.sum(member, axis=1, keepdims=True)
        c = r >> 1
        seg_mean = jnp.sum(member * token_logp[c : c + 1], axis=1, keepdims=True) / counts
        seg_ref = jnp.sum(jnp.where(seg_id == place, ref_rows[r], 0.0), axis=1, keepdims=True)
        hot = jnp.where(pair_rows[r] == seg_id, 1.0, 0.0)
        value = jnp.sum(hot * (seg_mean - seg_ref), axis=0, keepdims=True)
        pair = [value[:, k : k + 1] - value[:, k + 1 : k + 2] for k in range(0, places, 2)]
        margins = DPO_BETA * jnp.concatenate([p for p in pair for _ in range(2)], axis=1)
        down = -margins
        loss = jnp.maximum(down, 0.0) + jnp.log1p(jnp.exp(-jnp.abs(down)))
        losses.append(jnp.where(even, loss, 0.0))
        if r == 0:
            margins_out[...] = jnp.concatenate([DPO_BETA * p for p in pair], axis=1)
        if c == 0:
            pull = -(LOSS_SCALE / total_pairs) / (1.0 + jnp.exp(margins))
            pull = jnp.where(even, pull, -pull)
            seg_pull = DPO_BETA * jnp.sum(hot * pull, axis=1, keepdims=True) / counts
            weight = weight + jnp.sum(member * seg_pull, axis=0, keepdims=True)
    loss_out[...] = jnp.sum(tree_sum(losses), axis=1, keepdims=True) / total_pairs

    off = weight / exp_total[0:1]
    hit = off * others[0:1] * (1.0 - bent[0:1] * bent[0:1])
    dot = hit * raw_target[0:1] - off * pulled[0:1]
    scales[...] = jnp.concatenate([halves(off, off)[0], dot, jnp.zeros((6, LANES), jnp.float32)], axis=0)


def fold_half_kernel(mine, got, keep, send):
    rows = mine.shape[0] // 2
    for at in chunks(rows):
        low = after(at, rows)
        left, right = halves(wide(mine[at, :]) + wide(got[at, :]), wide(mine[low, :]) + wide(got[low, :]))
        keep[at, :] = left.astype(keep.dtype)
        send[at, :] = right.astype(send.dtype)


def join_kernel(first_row, mine, got, hit_mine, hit_got, sums, heard, left, right):
    total = sums[...] + heard[...]
    bent = jnp.tanh(total[2:3] / SOFTCAP)
    ratio = total[0:1] * (1.0 - bent * bent)
    ratio = jnp.where(whereabouts()[2] == 0, ratio, halves(ratio, ratio)[0])
    rows = mine.shape[0] // 2

    def joined(at):
        there = after(at, first_row)
        hit = wide(hit_mine[there, :]) + wide(hit_got[there, :])
        return ratio * hit - (mine[at, :] + wide(got[at, :]))

    for at in chunks(rows):
        near, away = halves(joined(at), joined(after(at, rows)))
        left[at, :] = near.astype(left.dtype)
        right[at, :] = away.astype(right.dtype)


def finish_kernel(width, mine, one, two, three, scales, inv_own, own_scale, hidden, out):
    tok = hidden.shape[0]
    grad = (mine[...] + wide(one[...])) + (wide(two[...]) + wide(three[...]))
    grad = (grad * scales[0:1, :] * own_scale[...]).T
    grad = jnp.concatenate([grad[:tok], grad[tok:]], axis=1)
    columns = jnp.concatenate([scales[1:2, :], inv_own[...], jnp.zeros((6, LANES), jnp.float32)], axis=0).T
    dot, inv = columns[:tok, 0:1], columns[:tok, 1:2]
    out[...] = inv * grad - wide(hidden[...]) * (dot * inv * inv / width)


def call(kernel, name, outs, in_specs, out_specs, scratch, limit, flops, moved, *args):
    return pl.pallas_call(
        kernel,
        out_shape=outs,
        in_specs=in_specs,
        out_specs=out_specs,
        scratch_shapes=scratch,
        compiler_params=pltpu.CompilerParams(vmem_limit_bytes=limit << 20),
        cost_estimate=pl.CostEstimate(flops=flops, bytes_accessed=moved, transcendentals=0),
        name=name,
    )(*args)


def fast_path(hidden, norm_gain, weight, targets, segment_ids, pairing, ref_logp):
    n_sec = lax.axis_size("section")
    n_dp = lax.axis_size("dp")
    n_z = n_sec // 2
    tok, cols = hidden.shape
    tokens = n_dp * tok
    width = cols * n_sec
    vocab = weight.shape[0]
    block = 2 * cols
    padded = -(-vocab // LANES) * LANES
    shape = jax.ShapeDtypeStruct
    half, full = jnp.bfloat16, jnp.float32

    def pairs(of):
        return [(s * n_dp + d, of(s, d)) for s in range(n_sec) for d in range(n_dp)]

    both_axes = ("section", "dp")
    one_pairs = pairs(lambda s, d: (s ^ 1) * n_dp + d if d & 1 == 0 else s * n_dp + (d ^ 2))
    two_pairs = pairs(lambda s, d: (s ^ 1) * n_dp + d if d & 1 == 1 else s * n_dp + (d ^ 2))
    to_one = lambda a: lax.ppermute(a, both_axes, one_pairs)
    to_two = lambda a: lax.ppermute(a, both_axes, two_pairs)
    over_core = lambda a: exchange(a, "dp", n_dp, 1)
    over_x = lambda a: exchange(a, "section", n_sec, 1)
    over_y = lambda a: exchange(a, "dp", n_dp, 2)
    over_z = lambda a, k: exchange(a, "section", n_sec, 2 * k)

    def hold(value, *others):
        return lax.optimization_barrier((value,) + others)[0]

    strips = [hidden] + [over_z(hidden, k) for k in range(1, n_z)]

    base = call(
        strips_kernel, "strips", shape((n_z * cols // 2, LANES), half), [VMEM] * n_z, VMEM, [], 4,
        tok * width, 0, *strips,
    )
    turned_a, turned_b, hit_keep, hit_send, flat = call(
        functools.partial(turn_kernel, cols, n_z), "turn_weight",
        (shape((width // 2, vocab), half),) * 2
        + (shape((width, LANES), half), shape((width, LANES), half), shape((1, tokens), jnp.int32)),
        [VMEM, VMEM], (VMEM,) * 5, [pltpu.VMEM((vocab, tokens), half)],
        8, 2 * tokens * vocab * width, 4 * vocab * width, hold(targets, base), weight,
    )

    one = to_one(base)
    two = to_two(base)
    table = call(
        gain_kernel, "gain_table", shape((width, LANES), full), [VMEM], VMEM, [], 4, width * LANES,
        16 * width * LANES, hold(norm_gain.reshape(-1, LANES), base),
    )
    half_rows = (shape((width // 2, LANES), half),) * 2
    hit_keep, hit_send = call(
        fold_core_kernel, "fold_rows", half_rows, [VMEM, VMEM], (VMEM, VMEM), [], 4,
        0, 96 * width * LANES, hit_keep, over_core(hold(hit_send, one, two)),
    )
    three = to_two(one)
    stacks = [base, one, two, three]
    stacks = stacks + [over_core(s) for s in (base, one, two, hold(three, hit_send, table))]
    hit_got = to_one(hold(hit_send, three, table))

    normed, inv_own, own_scale = call(
        functools.partial(norm_kernel, cols, n_z), "norm",
        (shape((width, tokens), half), shape((1, LANES), full), shape((cols // 2, LANES), full)),
        [VMEM] * 9, (VMEM,) * 3, [], 4, 8 * tokens * width, 0, *stacks, table,
    )
    raw_logits = lax.dot_general(
        weight, normed, (((1,), (0,)), ((), ())), preferred_element_type=jnp.float32
    )
    bent = jnp.tanh(raw_logits / SOFTCAP)
    hot = lax.broadcasted_iota(jnp.int32, (vocab, 1), 0) == flat
    power = jnp.where(hot, 0.0, jnp.exp(SOFTCAP * bent))
    sloped = power * (1.0 - bent * bent)
    stats = [
        jnp.sum(power, axis=0),
        jnp.sum(sloped * raw_logits, axis=0),
        jnp.sum(jnp.where(hot, raw_logits, 0.0), axis=0),
    ]
    stats = jnp.stack(stats)
    sloped = hold(sloped.astype(half), stats)

    def product(turned, sloped):
        return lax.dot_general(turned, sloped, (((1,), (0,)), ((), ())), preferred_element_type=full)

    def halved(kind, rows):
        return (shape((rows, LANES), kind), shape((rows, LANES), half))

    def fold(kernel, name, mine, got, kind=full):
        return call(
            kernel, name, halved(kind, mine.shape[0] // 2), [VMEM] * 2, (VMEM,) * 2, [], 4, 0, 0, mine, got
        )

    rows = width // 2
    grad_a = product(turned_a, sloped)
    send_a = call(post_kernel, "post", shape((rows, LANES), half), [VMEM], VMEM, [], 4, 0, 0, grad_a)
    got_a = over_core(send_a)
    sums = call(
        count_kernel, "count", shape((8, LANES), full), [VMEM] * 2, VMEM, [], 4, 0, 0, stats, over_core(stats)
    )
    grad_b = product(turned_b, hold(sloped, send_a, sums))
    sums = sums + over_x(sums)
    send_b = call(post_kernel, "post", shape((rows, LANES), half), [VMEM], VMEM, [], 4, 0, 0, hold(grad_b, sums))
    got_b = over_core(hold(send_b, hit_got))
    keep_a, send_a = fold(fold_core_kernel, "fold_core", grad_a, hold(got_a, sums))
    got_a = to_one(send_a)
    heard = over_y(sums)
    keep_b, send_b = fold(fold_core_kernel, "fold_core", grad_b, hold(got_b, send_a))
    got_b = to_one(send_b)
    sums = sums + jnp.concatenate([heard[:, HALF:], heard[:, :HALF]], axis=1)
    sums = sums + over_z(sums, 1)
    heard = over_z(sums, 2)

    rows = width // 4

    def join(name, first_row, mine, got):
        return call(
            functools.partial(join_kernel, first_row), name, halved(full, rows // 2),
            [VMEM] * 6, (VMEM,) * 2, [], 4, 0, 0, mine, got, hit_keep, hit_got, sums, heard,
        )

    keep_a, send_a = join("join_a", 0, keep_a, got_a)
    got_a = to_two(send_a)
    keep_b, send_b = join("join_b", rows, keep_b, hold(got_b, send_a))
    got_b = to_two(send_b)
    send_1, send_3 = fold(fold_half_kernel, "fold_last_a", keep_a, got_a, half)
    got_3 = over_z(send_3, 3)
    keep, send_2 = fold(fold_half_kernel, "fold_last_b", keep_b, hold(got_b, send_3))
    got_2, got_1 = over_z(send_2, 2), over_z(hold(send_1, send_2), 1)
    scales, margins, dpo_loss = call(
        tally_kernel, "tally",
        (shape((8, LANES), full), shape((1, ref_logp.shape[1] // 2), full), shape((1, 1), full)),
        [VMEM] * 5, (VMEM,) * 3, [], 4, 0, 0, sums, hold(heard, send_2), segment_ids, pairing, ref_logp,
    )
    hidden_grad = call(
        functools.partial(finish_kernel, width), "finish", shape((tok, cols), full),
        [VMEM] * 8, VMEM, [], 4, 0, 0,
        keep, got_1, got_2, got_3, scales, inv_own, own_scale, hidden,
    )
    return (hidden_grad, margins, dpo_loss.reshape(()))


def per_device(hidden, norm_gain, weight, *rest):
    n_sec, n_dp = lax.axis_size("section"), lax.axis_size("dp")
    tok, cols = hidden.shape
    vocab = weight.shape[0]
    fits = n_dp == 4 and n_sec == 8 and tok == HALF and cols % HALF == 0 and vocab % 8 == 0
    fits = fits and norm_gain.shape[0] % LANES == 0
    path = fast_path if fits else general_path
    return path(hidden, norm_gain, weight, *rest)


def solution(mesh):
    in_specs = (P("dp", "section"), P(), P(("section", "dp"), None), P(), P(), P(), P())
    out_specs = (P("dp", "section"), P("dp", None), P())
    return jax.shard_map(
        per_device, mesh=mesh, in_specs=in_specs, out_specs=out_specs, check_vma=False
    )
```

```python
import functools

import jax
import jax.numpy as jnp
from jax import lax
from jax.experimental import pallas as pl
from jax.experimental.pallas import tpu as pltpu
from jax.sharding import PartitionSpec as P

SOFTCAP = 30.0
DPO_BETA = 0.5
LOSS_SCALE = 65536.0
EPSILON = 1e-06


def swap_bits(arr, index, axis):
    count = arr.shape[axis]
    bit = 1
    while bit < count:
        shape = arr.shape[:axis] + (count // (2 * bit), 2, bit) + arr.shape[axis + 1 :]
        swapped = jnp.flip(arr.reshape(shape), axis + 1).reshape(arr.shape)
        arr = jnp.where((index & bit) != 0, swapped, arr)
        bit *= 2
    return arr


def exchange(arr, axis, size, mask):
    return lax.ppermute(arr, axis, [(i, i ^ mask) for i in range(size)])


def tree_sum(items):
    items = list(items)
    while len(items) > 1:
        items = [items[i] + items[i + 1] for i in range(0, len(items), 2)]
    return items[0]


def dpo_terms(token_logp, segment_ids, pairing, ref_logp):
    num_groups, group_tokens = segment_ids.shape
    seg_count = pairing.shape[1]
    pair_count = seg_count // 2
    logp_rows = token_logp.reshape(num_groups, group_tokens)
    seg_range = jnp.arange(seg_count, dtype=jnp.int32)
    member = (segment_ids[:, :, None] == seg_range[None, None, :]).astype(jnp.float32)
    counts = jnp.sum(member, axis=1)
    seg_mean = jnp.sum(member * logp_rows[:, :, None], axis=1) / counts
    adjusted = seg_mean - ref_logp
    chosen_hot = (pairing[:, 0::2, None] == seg_range[None, None, :]).astype(jnp.float32)
    rejected_hot = (pairing[:, 1::2, None] == seg_range[None, None, :]).astype(jnp.float32)
    chosen = jnp.sum(chosen_hot * adjusted[:, None, :], axis=2)
    rejected = jnp.sum(rejected_hot * adjusted[:, None, :], axis=2)
    margins = DPO_BETA * (chosen - rejected)
    losses = jax.nn.softplus(-margins)
    dpo_loss = jnp.sum(tree_sum([losses[k] for k in range(num_groups)])) / (num_groups * pair_count)
    margin_pull = -jax.nn.sigmoid(-margins) * (LOSS_SCALE / (num_groups * pair_count))
    seg_pull = (
        DPO_BETA * jnp.sum((chosen_hot - rejected_hot) * margin_pull[:, :, None], axis=1) / counts
    )
    token_weight = jnp.sum(member * seg_pull[:, None, :], axis=2).reshape(-1)
    return (margins, dpo_loss, token_weight)


def general_path(hidden, norm_gain, weight, targets, segment_ids, pairing, ref_logp):
    n_sec = lax.axis_size("section")
    n_dp = lax.axis_size("dp")
    n_z, n_y = n_sec // 2, n_dp // 2
    sec = lax.axis_index("section")
    dp = lax.axis_index("dp")
    z, x = sec >> 1, sec & 1
    tok, cols = hidden.shape
    half = tok // 2
    width = cols * n_sec
    vocab_rows = weight.shape[0]
    gain_scale = 1.0 + norm_gain
    own_scale = lax.dynamic_slice_in_dim(gain_scale, sec * cols, cols)

    over_core = lambda a: exchange(a, "dp", n_dp, 1)
    over_x = lambda a: exchange(a, "section", n_sec, 1)
    over_y = lambda a, k: exchange(a, "dp", n_dp, 2 * k)
    over_z = lambda a, k: exchange(a, "section", n_sec, 2 * k)

    targets = swap_bits(targets, dp, 0)
    segment_ids = swap_bits(segment_ids, dp, 0)
    pairing = swap_bits(pairing, dp, 0)
    ref_logp = swap_bits(ref_logp, dp, 0)

    def join_x(mine):
        other = over_x(mine)
        first = x == 0
        both = jnp.stack([jnp.where(first, mine, other), jnp.where(first, other, mine)], axis=-2)
        return both.reshape(both.shape[:-3] + (width,))

    pieces = jnp.stack([hidden] + [over_z(hidden, k) for k in range(1, n_z)], axis=1)
    pieces = swap_bits(pieces, z, 1)
    rows_a = join_x(pieces[:half])
    rows_a = jnp.stack([rows_a] + [over_y(rows_a, k) for k in range(1, n_y)])
    raw_b = pieces[half:]
    raw_b = jnp.stack([raw_b] + [over_y(raw_b, k) for k in range(1, n_y)])
    rows_b = join_x(raw_b)
    rows = jnp.concatenate([rows_a, rows_b], axis=1)
    rows = jnp.stack([rows, over_core(rows)], axis=1).reshape(n_dp * tok, width)

    rows32 = rows.astype(jnp.float32)
    inv_rms = lax.rsqrt(jnp.mean(rows32 * rows32, axis=1) + EPSILON)
    normed = (rows32 * inv_rms[:, None] * gain_scale[None, :]).astype(jnp.bfloat16)
    raw_logits = lax.dot_general(
        weight, normed, (((1,), (1,)), ((), ())), preferred_element_type=jnp.float32
    )
    bent = jnp.tanh(raw_logits / SOFTCAP)
    capped = SOFTCAP * bent
    cap_slope = 1.0 - bent * bent
    vocab_start = (sec * n_dp + dp) * vocab_rows
    vocab_ids = vocab_start + lax.broadcasted_iota(jnp.int32, (vocab_rows, 1), 0)
    target_hot = vocab_ids == targets.reshape(-1)[None, :]
    exp_logits = jnp.where(target_hot, 0.0, jnp.exp(capped))
    sums = jnp.stack(
        [
            jnp.sum(exp_logits, axis=0),
            jnp.sum(exp_logits * cap_slope * raw_logits, axis=0),
            jnp.sum(jnp.where(target_hot, raw_logits, 0.0), axis=0),
        ]
    )
    sums = swap_bits(sums.reshape(3, n_dp, tok), dp, 1)
    sums = sums + over_core(sums)
    sums = tree_sum([sums] + [over_y(sums, k) for k in range(1, n_y)])
    sums = sums + over_x(sums)
    sums = tree_sum([sums] + [over_z(sums, k) for k in range(1, n_z)])
    sums = swap_bits(sums, dp, 1).reshape(3, n_dp * tok)
    others, pulled, raw_target = sums[0], sums[1], sums[2]

    bent_target = jnp.tanh(raw_target / SOFTCAP)
    capped_target = SOFTCAP * bent_target
    exp_total = others + jnp.exp(capped_target)
    token_logp = capped_target - jnp.log(exp_total)
    margins, dpo_loss, token_weight = dpo_terms(token_logp, segment_ids, pairing, ref_logp)
    off_scale = token_weight / exp_total
    hit_scale = off_scale * others
    dlogit = (
        jnp.where(target_hot, hit_scale[None, :], -off_scale[None, :] * exp_logits) * cap_slope
    ).astype(jnp.bfloat16)
    row_dot_inv = hit_scale * (1.0 - bent_target * bent_target) * raw_target - off_scale * pulled

    grad = lax.dot_general(
        dlogit, weight, (((0,), (0,)), ((), ())), preferred_element_type=jnp.float32
    )

    def send(fn, arr, *args):
        return fn(arr.astype(jnp.bfloat16), *args).astype(jnp.float32)

    def split_x(arr):
        arr = arr.reshape(arr.shape[:-1] + (n_z, 2, cols))
        first = x == 0
        lo, hi = arr[..., 0, :], arr[..., 1, :]
        return jnp.where(first, lo, hi) + send(over_x, jnp.where(first, hi, lo))

    def split_y(arr):
        return tree_sum([arr[0]] + [send(over_y, arr[k], k) for k in range(1, n_y)])

    grad = grad.reshape(n_y, 2, tok, width)
    grad = grad[:, 0] + send(over_core, grad[:, 1])
    grad_a = split_y(split_x(grad[:, :half]))
    grad_b = split_x(split_y(grad[:, half:]))
    grad = jnp.moveaxis(jnp.concatenate([grad_a, grad_b], axis=0), 1, 0)
    grad = swap_bits(grad, z, 0)
    grad = tree_sum([grad[0]] + [send(over_z, grad[k], k) for k in range(1, n_z)])

    own_inv = inv_rms[:tok]
    hidden_grad = (
        own_scale[None, :] * own_inv[:, None] * grad
        - hidden.astype(jnp.float32) * (row_dot_inv[:tok] * own_inv * own_inv / width)[:, None]
    )
    return (hidden_grad, margins[:1], dpo_loss)


LANES = 128
HALF = LANES // 2
VMEM = pl.BlockSpec(memory_space=pltpu.VMEM)


def halves(a, b):
    lane = lax.broadcasted_iota(jnp.int32, a.shape, 1)
    crossed = pltpu.roll(jnp.where(lane < HALF, b, a), HALF, 1)
    return jnp.where(lane < HALF, a, crossed), jnp.where(lane < HALF, crossed, b)


def whereabouts():
    sec, dp = lax.axis_index("section"), lax.axis_index("dp")
    return sec >> 1, sec & 1, dp & 1, dp, sec * lax.axis_size("dp") + dp


def relative_rows(ids):
    dp = whereabouts()[3]
    return [ids[pl.ds(dp ^ ((r & 1) * 2 + (r >> 1)), 1), :] for r in range(4)]


def turn_kernel(cols, n_z, flat, weight, turned_a, turned_b, keep, send, hot):
    z, x, _, _, _ = whereabouts()
    vocab = weight.shape[0]
    block = 2 * cols
    row = lax.broadcasted_iota(jnp.int32, hot.shape, 0)
    hot[...] = jnp.where(row == flat[...], 1.0, 0.0).astype(jnp.bfloat16)
    for k in range(n_z):
        at = pl.multiple_of((z ^ k) * block, LANES)
        strip = [weight[:, pl.ds(at + c, LANES)].T for c in range(0, block, LANES)]
        strip = jnp.concatenate(strip, axis=0)
        turned = turned_a if k & 1 else turned_b
        for side in range(2):
            part = strip[side * cols : (side + 1) * cols, :]
            here = pl.multiple_of(((x ^ side) * (n_z // 2) + (k >> 1)) * cols, HALF)
            turned[pl.ds(here, cols), :] = part
            rows = lax.dot_general(
                part, hot[...], (((1,), (0,)), ((), ())), preferred_element_type=jnp.float32
            ).astype(jnp.bfloat16)
            here = pl.multiple_of(((x ^ side) * n_z + (k >> 1) + (0 if k & 1 else n_z // 2)) * cols, HALF)
            keep[pl.ds(here, cols), :] = rows[:, :LANES]
            send[pl.ds(here, cols), :] = rows[:, LANES:]


def flip(strip):
    flipped = wide(strip).T
    rows = flipped.shape[0] // 2
    return jnp.concatenate([flipped[:rows], flipped[rows:]], axis=1).astype(jnp.bfloat16)


def own_strip_kernel(vocab, strip, targets, out, flat):
    out[...] = flip(strip[...])
    flat[...] = jnp.concatenate(relative_rows(targets), axis=1) - whereabouts()[4] * vocab


def strips_kernel(own, *refs):
    strips, out = refs[:-1], refs[-1]
    rows = own.shape[0]
    out[:rows, :] = own[...]
    for k, strip in enumerate(strips):
        out[(k + 1) * rows : (k + 2) * rows, :] = flip(strip[...])


def gain_kernel(gain, table):
    for i in range(gain.shape[0]):
        row = jnp.broadcast_to(1.0 + gain[i : i + 1, :], (LANES, LANES))
        table[i * LANES : (i + 1) * LANES, :] = row.T


def norm_kernel(cols, n_z, *refs):
    stacks, table, normed, inv_own, own_scale = refs[:8], refs[8], refs[9], refs[10], refs[11]
    z, x, core, _, _ = whereabouts()
    rows = cols // 2
    own = pl.multiple_of((z * 2 + x) * cols, HALF)
    upper = table[pl.ds(pl.multiple_of(own + rows, 32), rows), :]
    own_scale[...] = halves(table[pl.ds(own, rows), :], upper)[0]
    width = normed.shape[0]
    lane = lax.broadcasted_iota(jnp.int32, (1, LANES), 1)

    def piece(ref, k):
        return wide(ref[k * rows : (k + 1) * rows, :])

    def squares(ref):
        parts = [piece(ref, k) for k in range(n_z)]
        return sum(jnp.sum(part * part, axis=0, keepdims=True) for part in parts)

    invs = []
    for far in range(2):
        base, one, two, three = stacks[4 * far : 4 * far + 4]
        x_first = core == far
        near, away = squares(base), squares(three)
        first, second = squares(one), squares(two)
        near = near + jnp.where(x_first, first, second)
        away = away + jnp.where(x_first, second, first)
        inv = [lax.rsqrt((sq + pltpu.roll(sq, HALF, 1)) / width + EPSILON) for sq in (near, away)]
        invs.append(jnp.where(lane < HALF, inv[0], inv[1]))
    inv_own[...] = invs[0]
    for k in range(n_z):
        for side in range(2):
            at = ((z ^ k) * 2 + (x ^ side)) * cols
            for far in range(2):
                base, one, two, three = stacks[4 * far : 4 * far + 4]
                x_first = core == far
                first, second = piece(one, k), piece(two, k)
                if side == 0:
                    near, away = piece(base, k), jnp.where(x_first, second, first)
                else:
                    near, away = jnp.where(x_first, first, second), piece(three, k)
                for part, value in enumerate(halves(near, away)):
                    here = pl.ds(pl.multiple_of(at + part * rows, 32), rows)
                    value = value * invs[far] * table[here, :]
                    normed[here, far * LANES : (far + 1) * LANES] = value.astype(jnp.bfloat16)


def post_kernel(grad, send):
    for at in chunks(grad.shape[0]):
        send[at, :] = grad[at, LANES:].astype(send.dtype)


def count_kernel(stats, got, sums):
    mine, theirs = stats[...], got[...]
    total = [mine[:, :LANES] + theirs[:, LANES:], mine[:, LANES:] + theirs[:, :LANES]]
    sums[...] = jnp.concatenate(total + [jnp.zeros((2, LANES), jnp.float32)], axis=0)


def chunks(rows):
    count = next(n for n in (8, 4, 2, 1) if rows % (16 * n) == 0)
    step = rows // count
    return [slice(i * step, (i + 1) * step) for i in range(count)]


def after(at, rows):
    return slice(at.start + rows, at.stop + rows)


def wide(a):
    return a.astype(jnp.float32)


def fold_core_kernel(mine, got, keep, send):
    rows = mine.shape[0] // 2

    def split(one_side):
        for at in chunks(rows):
            top = wide(mine[at, :LANES]) + wide(got[at, :])
            low = after(at, rows)
            bottom = wide(mine[low, :LANES]) + wide(got[low, :])
            if not one_side:
                top, bottom = halves(top, bottom)
            keep[at, :] = top.astype(keep.dtype)
            send[at, :] = bottom.astype(send.dtype)

    core = whereabouts()[2]
    pl.when(core == 0)(lambda: split(True))
    pl.when(core != 0)(lambda: split(False))


def tally_kernel(sums, heard, segments, pairing, ref_logp, scales, margins_out, loss_out):
    sums = sums[...] + heard[...]
    groups, places = pairing.shape
    total_pairs = groups * places // 2

    def both(i):
        return jnp.concatenate([sums[i : i + 1], sums[i + 3 : i + 4]], axis=0)

    others, pulled, raw_target = both(0), both(1), both(2)
    bent = jnp.tanh(raw_target / SOFTCAP)
    capped = SOFTCAP * bent
    exp_total = others + jnp.exp(capped)
    token_logp = capped - jnp.log(exp_total)

    seg_rows, pair_rows, ref_rows = relative_rows(segments), relative_rows(pairing), relative_rows(ref_logp)
    seg_id = lax.broadcasted_iota(jnp.int32, (places, places), 0)
    place = lax.broadcasted_iota(jnp.int32, (places, places), 1)
    even = (place[0:1] & 1) == 0
    lane = lax.broadcasted_iota(jnp.int32, (1, LANES), 1)
    losses, weight = [], jnp.zeros((1, LANES), jnp.float32)
    for r in range(groups):
        seg = jnp.concatenate([seg_rows[r & 2], seg_rows[(r & 2) + 1]], axis=1)
        inside = jnp.logical_and(seg == seg_id[:, 0:1], (lane >= HALF) == ((r & 1) == 1))
        member = jnp.where(inside, 1.0, 0.0)
        counts = jnp.sum(member, axis=1, keepdims=True)
        c = r >> 1
        seg_mean = jnp.sum(member * token_logp[c : c + 1], axis=1, keepdims=True) / counts
        seg_ref = jnp.sum(jnp.where(seg_id == place, ref_rows[r], 0.0), axis=1, keepdims=True)
        hot = jnp.where(pair_rows[r] == seg_id, 1.0, 0.0)
        value = jnp.sum(hot * (seg_mean - seg_ref), axis=0, keepdims=True)
        pair = [value[:, k : k + 1] - value[:, k + 1 : k + 2] for k in range(0, places, 2)]
        margins = DPO_BETA * jnp.concatenate([p for p in pair for _ in range(2)], axis=1)
        down = -margins
        loss = jnp.maximum(down, 0.0) + jnp.log1p(jnp.exp(-jnp.abs(down)))
        losses.append(jnp.where(even, loss, 0.0))
        if r == 0:
            margins_out[...] = jnp.concatenate([DPO_BETA * p for p in pair], axis=1)
        if c == 0:
            pull = -(LOSS_SCALE / total_pairs) / (1.0 + jnp.exp(margins))
            pull = jnp.where(even, pull, -pull)
            seg_pull = DPO_BETA * jnp.sum(hot * pull, axis=1, keepdims=True) / counts
            weight = weight + jnp.sum(member * seg_pull, axis=0, keepdims=True)
    loss_out[...] = jnp.sum(tree_sum(losses), axis=1, keepdims=True) / total_pairs

    off = weight / exp_total[0:1]
    hit = off * others[0:1] * (1.0 - bent[0:1] * bent[0:1])
    dot = hit * raw_target[0:1] - off * pulled[0:1]
    scales[...] = jnp.concatenate([halves(off, off)[0], dot, jnp.zeros((6, LANES), jnp.float32)], axis=0)


def fold_half_kernel(mine, got, keep, send):
    rows = mine.shape[0] // 2
    for at in chunks(rows):
        low = after(at, rows)
        left, right = halves(wide(mine[at, :]) + wide(got[at, :]), wide(mine[low, :]) + wide(got[low, :]))
        keep[at, :] = left.astype(keep.dtype)
        send[at, :] = right.astype(send.dtype)


def join_kernel(first_row, mine, got, hit_mine, hit_got, sums, heard, left, right):
    total = sums[...] + heard[...]
    bent = jnp.tanh(total[2:3] / SOFTCAP)
    ratio = total[0:1] * (1.0 - bent * bent)
    ratio = jnp.where(whereabouts()[2] == 0, ratio, halves(ratio, ratio)[0])
    rows = mine.shape[0] // 2

    def joined(at):
        there = after(at, first_row)
        hit = wide(hit_mine[there, :]) + wide(hit_got[there, :])
        return ratio * hit - (mine[at, :] + wide(got[at, :]))

    for at in chunks(rows):
        near, away = halves(joined(at), joined(after(at, rows)))
        left[at, :] = near.astype(left.dtype)
        right[at, :] = away.astype(right.dtype)


def finish_kernel(width, mine, one, two, three, scales, inv_own, own_scale, hidden, out):
    tok = hidden.shape[0]
    grad = (mine[...] + wide(one[...])) + (wide(two[...]) + wide(three[...]))
    grad = (grad * scales[0:1, :] * own_scale[...]).T
    grad = jnp.concatenate([grad[:tok], grad[tok:]], axis=1)
    columns = jnp.concatenate([scales[1:2, :], inv_own[...], jnp.zeros((6, LANES), jnp.float32)], axis=0).T
    dot, inv = columns[:tok, 0:1], columns[:tok, 1:2]
    out[...] = inv * grad - wide(hidden[...]) * (dot * inv * inv / width)


def call(kernel, name, outs, in_specs, out_specs, scratch, limit, flops, moved, *args):
    return pl.pallas_call(
        kernel,
        out_shape=outs,
        in_specs=in_specs,
        out_specs=out_specs,
        scratch_shapes=scratch,
        compiler_params=pltpu.CompilerParams(vmem_limit_bytes=limit << 20),
        cost_estimate=pl.CostEstimate(flops=flops, bytes_accessed=moved, transcendentals=0),
        name=name,
    )(*args)


def fast_path(hidden, norm_gain, weight, targets, segment_ids, pairing, ref_logp):
    n_sec = lax.axis_size("section")
    n_dp = lax.axis_size("dp")
    n_z = n_sec // 2
    tok, cols = hidden.shape
    tokens = n_dp * tok
    width = cols * n_sec
    vocab = weight.shape[0]
    block = 2 * cols
    padded = -(-vocab // LANES) * LANES
    shape = jax.ShapeDtypeStruct
    half, full = jnp.bfloat16, jnp.float32

    def pairs(of):
        return [(s * n_dp + d, of(s, d)) for s in range(n_sec) for d in range(n_dp)]

    both_axes = ("section", "dp")
    one_pairs = pairs(lambda s, d: (s ^ 1) * n_dp + d if d & 1 == 0 else s * n_dp + (d ^ 2))
    two_pairs = pairs(lambda s, d: (s ^ 1) * n_dp + d if d & 1 == 1 else s * n_dp + (d ^ 2))
    to_one = lambda a: lax.ppermute(a, both_axes, one_pairs)
    to_two = lambda a: lax.ppermute(a, both_axes, two_pairs)
    over_core = lambda a: exchange(a, "dp", n_dp, 1)
    over_x = lambda a: exchange(a, "section", n_sec, 1)
    over_y = lambda a: exchange(a, "dp", n_dp, 2)
    over_z = lambda a, k: exchange(a, "section", n_sec, 2 * k)

    def hold(value, *others):
        return lax.optimization_barrier((value,) + others)[0]

    strips = [hidden] + [over_z(hidden, k) for k in range(1, n_z)]

    strips[0], flat = call(
        functools.partial(own_strip_kernel, vocab), "own_strip",
        (shape((cols // 2, LANES), half), shape((1, tokens), jnp.int32)),
        [VMEM, VMEM], (VMEM, VMEM), [], 4, 0, 16 * width * LANES, hidden, targets,
    )
    base = call(
        strips_kernel, "strips", shape((n_z * cols // 2, LANES), half), [VMEM] * n_z, VMEM, [], 4,
        tok * width, 0, *strips,
    )
    turned_a, turned_b, hit_keep, hit_send = call(
        functools.partial(turn_kernel, cols, n_z), "turn_weight",
        (shape((width // 2, vocab), half),) * 2
        + (shape((width, LANES), half),) * 2,
        [VMEM, VMEM], (VMEM,) * 4, [pltpu.VMEM((vocab, tokens), half)],
        8, 2 * tokens * vocab * width, 4 * vocab * width, hold(flat, base), weight,
    )

    one = to_one(base)
    two = to_two(base)
    table = call(
        gain_kernel, "gain_table", shape((width, LANES), full), [VMEM], VMEM, [], 4, width * LANES,
        16 * width * LANES, hold(norm_gain.reshape(-1, LANES), base),
    )
    half_rows = (shape((width // 2, LANES), half),) * 2
    hit_keep, hit_send = call(
        fold_core_kernel, "fold_rows", half_rows, [VMEM, VMEM], (VMEM, VMEM), [], 4,
        0, 96 * width * LANES, hit_keep, over_core(hold(hit_send, one, two)),
    )
    three = to_two(one)
    stacks = [base, one, two, three]
    stacks = stacks + [over_core(s) for s in (base, one, two, hold(three, hit_send, table))]
    hit_got = to_one(hold(hit_send, three, table))

    normed, inv_own, own_scale = call(
        functools.partial(norm_kernel, cols, n_z), "norm",
        (shape((width, tokens), half), shape((1, LANES), full), shape((cols // 2, LANES), full)),
        [VMEM] * 9, (VMEM,) * 3, [], 4, 8 * tokens * width, 0, *stacks, table,
    )
    raw_logits = lax.dot_general(
        weight, normed, (((1,), (0,)), ((), ())), preferred_element_type=jnp.float32
    )
    bent = jnp.tanh(raw_logits / SOFTCAP)
    hot = lax.broadcasted_iota(jnp.int32, (vocab, 1), 0) == flat
    power = jnp.where(hot, 0.0, jnp.exp(SOFTCAP * bent))
    sloped = power * (1.0 - bent * bent)
    stats = [
        jnp.sum(power, axis=0),
        jnp.sum(sloped * raw_logits, axis=0),
        jnp.sum(jnp.where(hot, raw_logits, 0.0), axis=0),
    ]
    stats = jnp.stack(stats)
    sloped = hold(sloped.astype(half), stats)

    def product(turned, sloped):
        return lax.dot_general(turned, sloped, (((1,), (0,)), ((), ())), preferred_element_type=full)

    def halved(kind, rows):
        return (shape((rows, LANES), kind), shape((rows, LANES), half))

    def fold(kernel, name, mine, got, kind=full):
        return call(
            kernel, name, halved(kind, mine.shape[0] // 2), [VMEM] * 2, (VMEM,) * 2, [], 4, 0, 0, mine, got
        )

    rows = width // 2
    grad_a = product(turned_a, sloped)
    send_a = call(post_kernel, "post", shape((rows, LANES), half), [VMEM], VMEM, [], 4, 0, 0, grad_a)
    got_a = over_core(send_a)
    sums = call(
        count_kernel, "count", shape((8, LANES), full), [VMEM] * 2, VMEM, [], 4, 0, 0, stats, over_core(stats)
    )
    grad_b = product(turned_b, hold(sloped, send_a, sums))
    sums = sums + over_x(sums)
    send_b = call(post_kernel, "post", shape((rows, LANES), half), [VMEM], VMEM, [], 4, 0, 0, hold(grad_b, sums))
    got_b = over_core(hold(send_b, hit_got))
    keep_a, send_a = fold(fold_core_kernel, "fold_core", grad_a, hold(got_a, sums))
    got_a = to_one(send_a)
    heard = over_y(sums)
    keep_b, send_b = fold(fold_core_kernel, "fold_core", grad_b, hold(got_b, send_a))
    got_b = to_one(send_b)
    sums = sums + jnp.concatenate([heard[:, HALF:], heard[:, :HALF]], axis=1)
    sums = sums + over_z(sums, 1)
    heard = over_z(sums, 2)

    rows = width // 4

    def join(name, first_row, mine, got):
        return call(
            functools.partial(join_kernel, first_row), name, halved(full, rows // 2),
            [VMEM] * 6, (VMEM,) * 2, [], 4, 0, 0, mine, got, hit_keep, hit_got, sums, heard,
        )

    keep_a, send_a = join("join_a", 0, keep_a, got_a)
    got_a = to_two(send_a)
    keep_b, send_b = join("join_b", rows, keep_b, hold(got_b, send_a))
    got_b = to_two(send_b)
    send_1, send_3 = fold(fold_half_kernel, "fold_last_a", keep_a, got_a, half)
    got_3 = over_z(send_3, 3)
    keep, send_2 = fold(fold_half_kernel, "fold_last_b", keep_b, hold(got_b, send_3))
    got_2, got_1 = over_z(send_2, 2), over_z(hold(send_1, send_2), 1)
    scales, margins, dpo_loss = call(
        tally_kernel, "tally",
        (shape((8, LANES), full), shape((1, ref_logp.shape[1] // 2), full), shape((1, 1), full)),
        [VMEM] * 5, (VMEM,) * 3, [], 4, 0, 0, sums, hold(heard, send_2), segment_ids, pairing, ref_logp,
    )
    hidden_grad = call(
        functools.partial(finish_kernel, width), "finish", shape((tok, cols), full),
        [VMEM] * 8, VMEM, [], 4, 0, 0,
        keep, got_1, got_2, got_3, scales, inv_own, own_scale, hidden,
    )
    return (hidden_grad, margins, dpo_loss.reshape(()))


def per_device(hidden, norm_gain, weight, *rest):
    n_sec, n_dp = lax.axis_size("section"), lax.axis_size("dp")
    tok, cols = hidden.shape
    vocab = weight.shape[0]
    fits = n_dp == 4 and n_sec == 8 and tok == HALF and cols % HALF == 0 and vocab % 8 == 0
    fits = fits and norm_gain.shape[0] % LANES == 0
    path = fast_path if fits else general_path
    return path(hidden, norm_gain, weight, *rest)


def solution(mesh):
    in_specs = (P("dp", "section"), P(), P(("section", "dp"), None), P(), P(), P(), P())
    out_specs = (P("dp", "section"), P("dp", None), P())
    return jax.shard_map(
        per_device, mesh=mesh, in_specs=in_specs, out_specs=out_specs, check_vma=False
    )
```

```python
import functools

import jax
import jax.numpy as jnp
from jax import lax
from jax.experimental import pallas as pl
from jax.experimental.pallas import tpu as pltpu
from jax.sharding import PartitionSpec as P

SOFTCAP = 30.0
DPO_BETA = 0.5
LOSS_SCALE = 65536.0
EPSILON = 1e-06


def swap_bits(arr, index, axis):
    count = arr.shape[axis]
    bit = 1
    while bit < count:
        shape = arr.shape[:axis] + (count // (2 * bit), 2, bit) + arr.shape[axis + 1 :]
        swapped = jnp.flip(arr.reshape(shape), axis + 1).reshape(arr.shape)
        arr = jnp.where((index & bit) != 0, swapped, arr)
        bit *= 2
    return arr


def exchange(arr, axis, size, mask):
    return lax.ppermute(arr, axis, [(i, i ^ mask) for i in range(size)])


def tree_sum(items):
    items = list(items)
    while len(items) > 1:
        items = [items[i] + items[i + 1] for i in range(0, len(items), 2)]
    return items[0]


def dpo_terms(token_logp, segment_ids, pairing, ref_logp):
    num_groups, group_tokens = segment_ids.shape
    seg_count = pairing.shape[1]
    pair_count = seg_count // 2
    logp_rows = token_logp.reshape(num_groups, group_tokens)
    seg_range = jnp.arange(seg_count, dtype=jnp.int32)
    member = (segment_ids[:, :, None] == seg_range[None, None, :]).astype(jnp.float32)
    counts = jnp.sum(member, axis=1)
    seg_mean = jnp.sum(member * logp_rows[:, :, None], axis=1) / counts
    adjusted = seg_mean - ref_logp
    chosen_hot = (pairing[:, 0::2, None] == seg_range[None, None, :]).astype(jnp.float32)
    rejected_hot = (pairing[:, 1::2, None] == seg_range[None, None, :]).astype(jnp.float32)
    chosen = jnp.sum(chosen_hot * adjusted[:, None, :], axis=2)
    rejected = jnp.sum(rejected_hot * adjusted[:, None, :], axis=2)
    margins = DPO_BETA * (chosen - rejected)
    losses = jax.nn.softplus(-margins)
    dpo_loss = jnp.sum(tree_sum([losses[k] for k in range(num_groups)])) / (num_groups * pair_count)
    margin_pull = -jax.nn.sigmoid(-margins) * (LOSS_SCALE / (num_groups * pair_count))
    seg_pull = (
        DPO_BETA * jnp.sum((chosen_hot - rejected_hot) * margin_pull[:, :, None], axis=1) / counts
    )
    token_weight = jnp.sum(member * seg_pull[:, None, :], axis=2).reshape(-1)
    return (margins, dpo_loss, token_weight)


def general_path(hidden, norm_gain, weight, targets, segment_ids, pairing, ref_logp):
    n_sec = lax.axis_size("section")
    n_dp = lax.axis_size("dp")
    n_z, n_y = n_sec // 2, n_dp // 2
    sec = lax.axis_index("section")
    dp = lax.axis_index("dp")
    z, x = sec >> 1, sec & 1
    tok, cols = hidden.shape
    half = tok // 2
    width = cols * n_sec
    vocab_rows = weight.shape[0]
    gain_scale = 1.0 + norm_gain
    own_scale = lax.dynamic_slice_in_dim(gain_scale, sec * cols, cols)

    over_core = lambda a: exchange(a, "dp", n_dp, 1)
    over_x = lambda a: exchange(a, "section", n_sec, 1)
    over_y = lambda a, k: exchange(a, "dp", n_dp, 2 * k)
    over_z = lambda a, k: exchange(a, "section", n_sec, 2 * k)

    targets = swap_bits(targets, dp, 0)
    segment_ids = swap_bits(segment_ids, dp, 0)
    pairing = swap_bits(pairing, dp, 0)
    ref_logp = swap_bits(ref_logp, dp, 0)

    def join_x(mine):
        other = over_x(mine)
        first = x == 0
        both = jnp.stack([jnp.where(first, mine, other), jnp.where(first, other, mine)], axis=-2)
        return both.reshape(both.shape[:-3] + (width,))

    pieces = jnp.stack([hidden] + [over_z(hidden, k) for k in range(1, n_z)], axis=1)
    pieces = swap_bits(pieces, z, 1)
    rows_a = join_x(pieces[:half])
    rows_a = jnp.stack([rows_a] + [over_y(rows_a, k) for k in range(1, n_y)])
    raw_b = pieces[half:]
    raw_b = jnp.stack([raw_b] + [over_y(raw_b, k) for k in range(1, n_y)])
    rows_b = join_x(raw_b)
    rows = jnp.concatenate([rows_a, rows_b], axis=1)
    rows = jnp.stack([rows, over_core(rows)], axis=1).reshape(n_dp * tok, width)

    rows32 = rows.astype(jnp.float32)
    inv_rms = lax.rsqrt(jnp.mean(rows32 * rows32, axis=1) + EPSILON)
    normed = (rows32 * inv_rms[:, None] * gain_scale[None, :]).astype(jnp.bfloat16)
    raw_logits = lax.dot_general(
        weight, normed, (((1,), (1,)), ((), ())), preferred_element_type=jnp.float32
    )
    bent = jnp.tanh(raw_logits / SOFTCAP)
    capped = SOFTCAP * bent
    cap_slope = 1.0 - bent * bent
    vocab_start = (sec * n_dp + dp) * vocab_rows
    vocab_ids = vocab_start + lax.broadcasted_iota(jnp.int32, (vocab_rows, 1), 0)
    target_hot = vocab_ids == targets.reshape(-1)[None, :]
    exp_logits = jnp.where(target_hot, 0.0, jnp.exp(capped))
    sums = jnp.stack(
        [
            jnp.sum(exp_logits, axis=0),
            jnp.sum(exp_logits * cap_slope * raw_logits, axis=0),
            jnp.sum(jnp.where(target_hot, raw_logits, 0.0), axis=0),
        ]
    )
    sums = swap_bits(sums.reshape(3, n_dp, tok), dp, 1)
    sums = sums + over_core(sums)
    sums = tree_sum([sums] + [over_y(sums, k) for k in range(1, n_y)])
    sums = sums + over_x(sums)
    sums = tree_sum([sums] + [over_z(sums, k) for k in range(1, n_z)])
    sums = swap_bits(sums, dp, 1).reshape(3, n_dp * tok)
    others, pulled, raw_target = sums[0], sums[1], sums[2]

    bent_target = jnp.tanh(raw_target / SOFTCAP)
    capped_target = SOFTCAP * bent_target
    exp_total = others + jnp.exp(capped_target)
    token_logp = capped_target - jnp.log(exp_total)
    margins, dpo_loss, token_weight = dpo_terms(token_logp, segment_ids, pairing, ref_logp)
    off_scale = token_weight / exp_total
    hit_scale = off_scale * others
    dlogit = (
        jnp.where(target_hot, hit_scale[None, :], -off_scale[None, :] * exp_logits) * cap_slope
    ).astype(jnp.bfloat16)
    row_dot_inv = hit_scale * (1.0 - bent_target * bent_target) * raw_target - off_scale * pulled

    grad = lax.dot_general(
        dlogit, weight, (((0,), (0,)), ((), ())), preferred_element_type=jnp.float32
    )

    def send(fn, arr, *args):
        return fn(arr.astype(jnp.bfloat16), *args).astype(jnp.float32)

    def split_x(arr):
        arr = arr.reshape(arr.shape[:-1] + (n_z, 2, cols))
        first = x == 0
        lo, hi = arr[..., 0, :], arr[..., 1, :]
        return jnp.where(first, lo, hi) + send(over_x, jnp.where(first, hi, lo))

    def split_y(arr):
        return tree_sum([arr[0]] + [send(over_y, arr[k], k) for k in range(1, n_y)])

    grad = grad.reshape(n_y, 2, tok, width)
    grad = grad[:, 0] + send(over_core, grad[:, 1])
    grad_a = split_y(split_x(grad[:, :half]))
    grad_b = split_x(split_y(grad[:, half:]))
    grad = jnp.moveaxis(jnp.concatenate([grad_a, grad_b], axis=0), 1, 0)
    grad = swap_bits(grad, z, 0)
    grad = tree_sum([grad[0]] + [send(over_z, grad[k], k) for k in range(1, n_z)])

    own_inv = inv_rms[:tok]
    hidden_grad = (
        own_scale[None, :] * own_inv[:, None] * grad
        - hidden.astype(jnp.float32) * (row_dot_inv[:tok] * own_inv * own_inv / width)[:, None]
    )
    return (hidden_grad, margins[:1], dpo_loss)


LANES = 128
HALF = LANES // 2
VMEM = pl.BlockSpec(memory_space=pltpu.VMEM)


def halves(a, b):
    lane = lax.broadcasted_iota(jnp.int32, a.shape, 1)
    crossed = pltpu.roll(jnp.where(lane < HALF, b, a), HALF, 1)
    return jnp.where(lane < HALF, a, crossed), jnp.where(lane < HALF, crossed, b)


def whereabouts():
    sec, dp = lax.axis_index("section"), lax.axis_index("dp")
    return sec >> 1, sec & 1, dp & 1, dp, sec * lax.axis_size("dp") + dp


def relative_rows(ids):
    dp = whereabouts()[3]
    return [ids[pl.ds(dp ^ ((r & 1) * 2 + (r >> 1)), 1), :] for r in range(4)]


def turn_kernel(cols, n_z, flat, weight, turned_a, turned_b, keep, send, hot):
    z, x, _, _, _ = whereabouts()
    vocab = weight.shape[0]
    block = 2 * cols
    row = lax.broadcasted_iota(jnp.int32, hot.shape, 0)
    hot[...] = jnp.where(row == flat[...], 1.0, 0.0).astype(jnp.bfloat16)
    for k in range(n_z):
        at = pl.multiple_of((z ^ k) * block, LANES)
        strip = [weight[:, pl.ds(at + c, LANES)].T for c in range(0, block, LANES)]
        strip = jnp.concatenate(strip, axis=0)
        turned = turned_a if k & 1 else turned_b
        for side in range(2):
            part = strip[side * cols : (side + 1) * cols, :]
            here = pl.multiple_of(((x ^ side) * (n_z // 2) + (k >> 1)) * cols, HALF)
            turned[pl.ds(here, cols), :] = part
            rows = lax.dot_general(
                part, hot[...], (((1,), (0,)), ((), ())), preferred_element_type=jnp.float32
            ).astype(jnp.bfloat16)
            here = pl.multiple_of(((x ^ side) * n_z + (k >> 1) + (0 if k & 1 else n_z // 2)) * cols, HALF)
            keep[pl.ds(here, cols), :] = rows[:, :LANES]
            send[pl.ds(here, cols), :] = rows[:, LANES:]


def flip(strip):
    flipped = wide(strip).T
    rows = flipped.shape[0] // 2
    return jnp.concatenate([flipped[:rows], flipped[rows:]], axis=1).astype(jnp.bfloat16)


def own_strip_kernel(vocab, strip, targets, out, flat):
    out[...] = flip(strip[...])
    flat[...] = jnp.concatenate(relative_rows(targets), axis=1) - whereabouts()[4] * vocab


def strips_kernel(own, *refs):
    strips, out = refs[:-1], refs[-1]
    rows = own.shape[0]
    out[:rows, :] = own[...]
    for k, strip in enumerate(strips):
        out[(k + 1) * rows : (k + 2) * rows, :] = flip(strip[...])


def gain_kernel(gain, table):
    for i in range(gain.shape[0]):
        row = jnp.broadcast_to(1.0 + gain[i : i + 1, :], (LANES, LANES))
        table[i * LANES : (i + 1) * LANES, :] = row.T


def norm_kernel(cols, n_z, *refs):
    stacks, table, normed, inv_own, own_scale = refs[:8], refs[8], refs[9], refs[10], refs[11]
    z, x, core, _, _ = whereabouts()
    rows = cols // 2
    own = pl.multiple_of((z * 2 + x) * cols, HALF)
    upper = table[pl.ds(pl.multiple_of(own + rows, 32), rows), :]
    own_scale[...] = halves(table[pl.ds(own, rows), :], upper)[0]
    width = normed.shape[0]
    lane = lax.broadcasted_iota(jnp.int32, (1, LANES), 1)

    def piece(ref, k):
        return wide(ref[k * rows : (k + 1) * rows, :])

    def squares(ref):
        parts = [piece(ref, k) for k in range(n_z)]
        return sum(jnp.sum(part * part, axis=0, keepdims=True) for part in parts)

    invs = []
    for far in range(2):
        base, one, two, three = stacks[4 * far : 4 * far + 4]
        x_first = core == far
        near, away = squares(base), squares(three)
        first, second = squares(one), squares(two)
        near = near + jnp.where(x_first, first, second)
        away = away + jnp.where(x_first, second, first)
        inv = [lax.rsqrt((sq + pltpu.roll(sq, HALF, 1)) / width + EPSILON) for sq in (near, away)]
        invs.append(jnp.where(lane < HALF, inv[0], inv[1]))
    inv_own[...] = invs[0]
    for k in range(n_z):
        for side in range(2):
            at = ((z ^ k) * 2 + (x ^ side)) * cols
            for far in range(2):
                base, one, two, three = stacks[4 * far : 4 * far + 4]
                x_first = core == far
                first, second = piece(one, k), piece(two, k)
                if side == 0:
                    near, away = piece(base, k), jnp.where(x_first, second, first)
                else:
                    near, away = jnp.where(x_first, first, second), piece(three, k)
                for part, value in enumerate(halves(near, away)):
                    here = pl.ds(pl.multiple_of(at + part * rows, 32), rows)
                    value = value * invs[far] * table[here, :]
                    normed[here, far * LANES : (far + 1) * LANES] = value.astype(jnp.bfloat16)


def post_kernel(grad, send):
    for at in chunks(grad.shape[0]):
        send[at, :] = grad[at, LANES:].astype(send.dtype)


def count_kernel(stats, got, sums):
    mine, theirs = stats[...], got[...]
    total = [mine[:, :LANES] + theirs[:, LANES:], mine[:, LANES:] + theirs[:, :LANES]]
    sums[...] = jnp.concatenate(total + [jnp.zeros((2, LANES), jnp.float32)], axis=0)


def chunks(rows):
    count = next(n for n in (8, 4, 2, 1) if rows % (16 * n) == 0)
    step = rows // count
    return [slice(i * step, (i + 1) * step) for i in range(count)]


def after(at, rows):
    return slice(at.start + rows, at.stop + rows)


def wide(a):
    return a.astype(jnp.float32)


def fold_core_kernel(mine, got, keep, send):
    rows = mine.shape[0] // 2

    def split(one_side):
        for at in chunks(rows):
            top = wide(mine[at, :LANES]) + wide(got[at, :])
            low = after(at, rows)
            bottom = wide(mine[low, :LANES]) + wide(got[low, :])
            if not one_side:
                top, bottom = halves(top, bottom)
            keep[at, :] = top.astype(keep.dtype)
            send[at, :] = bottom.astype(send.dtype)

    core = whereabouts()[2]
    pl.when(core == 0)(lambda: split(True))
    pl.when(core != 0)(lambda: split(False))


def tally_kernel(sums, heard, segments, pairing, ref_logp, scales, margins_out, loss_out):
    sums = sums[...] + heard[...]
    groups, places = pairing.shape
    total_pairs = groups * places // 2

    def both(i):
        return jnp.concatenate([sums[i : i + 1], sums[i + 3 : i + 4]], axis=0)

    others, pulled, raw_target = both(0), both(1), both(2)
    bent = jnp.tanh(raw_target / SOFTCAP)
    capped = SOFTCAP * bent
    exp_total = others + jnp.exp(capped)
    token_logp = capped - jnp.log(exp_total)

    seg_rows, pair_rows, ref_rows = relative_rows(segments), relative_rows(pairing), relative_rows(ref_logp)
    seg_id = lax.broadcasted_iota(jnp.int32, (places, places), 0)
    place = lax.broadcasted_iota(jnp.int32, (places, places), 1)
    even = (place[0:1] & 1) == 0
    lane = lax.broadcasted_iota(jnp.int32, (1, LANES), 1)
    losses, weight = [], jnp.zeros((1, LANES), jnp.float32)
    for r in range(groups):
        seg = jnp.concatenate([seg_rows[r & 2], seg_rows[(r & 2) + 1]], axis=1)
        inside = jnp.logical_and(seg == seg_id[:, 0:1], (lane >= HALF) == ((r & 1) == 1))
        member = jnp.where(inside, 1.0, 0.0)
        counts = jnp.sum(member, axis=1, keepdims=True)
        c = r >> 1
        seg_mean = jnp.sum(member * token_logp[c : c + 1], axis=1, keepdims=True) / counts
        seg_ref = jnp.sum(jnp.where(seg_id == place, ref_rows[r], 0.0), axis=1, keepdims=True)
        hot = jnp.where(pair_rows[r] == seg_id, 1.0, 0.0)
        value = jnp.sum(hot * (seg_mean - seg_ref), axis=0, keepdims=True)
        pair = [value[:, k : k + 1] - value[:, k + 1 : k + 2] for k in range(0, places, 2)]
        margins = DPO_BETA * jnp.concatenate([p for p in pair for _ in range(2)], axis=1)
        down = -margins
        loss = jnp.maximum(down, 0.0) + jnp.log1p(jnp.exp(-jnp.abs(down)))
        losses.append(jnp.where(even, loss, 0.0))
        if r == 0:
            margins_out[...] = jnp.concatenate([DPO_BETA * p for p in pair], axis=1)
        if c == 0:
            pull = -(LOSS_SCALE / total_pairs) / (1.0 + jnp.exp(margins))
            pull = jnp.where(even, pull, -pull)
            seg_pull = DPO_BETA * jnp.sum(hot * pull, axis=1, keepdims=True) / counts
            weight = weight + jnp.sum(member * seg_pull, axis=0, keepdims=True)
    loss_out[...] = jnp.sum(tree_sum(losses), axis=1, keepdims=True) / total_pairs

    off = weight / exp_total[0:1]
    hit = off * others[0:1] * (1.0 - bent[0:1] * bent[0:1])
    dot = hit * raw_target[0:1] - off * pulled[0:1]
    scales[...] = jnp.concatenate([halves(off, off)[0], dot, jnp.zeros((6, LANES), jnp.float32)], axis=0)


def fold_half_kernel(mine, got, keep, send):
    rows = mine.shape[0] // 2
    for at in chunks(rows):
        low = after(at, rows)
        left, right = halves(wide(mine[at, :]) + wide(got[at, :]), wide(mine[low, :]) + wide(got[low, :]))
        keep[at, :] = left.astype(keep.dtype)
        send[at, :] = right.astype(send.dtype)


def join_kernel(first_row, mine, got, hit_mine, hit_got, sums, heard, left, right):
    total = sums[...] + heard[...]
    bent = jnp.tanh(total[2:3] / SOFTCAP)
    ratio = total[0:1] * (1.0 - bent * bent)
    ratio = jnp.where(whereabouts()[2] == 0, ratio, halves(ratio, ratio)[0])
    rows = mine.shape[0] // 2

    def joined(at):
        there = after(at, first_row)
        hit = wide(hit_mine[there, :]) + wide(hit_got[there, :])
        return ratio * hit - (mine[at, :] + wide(got[at, :]))

    for at in chunks(rows):
        near, away = halves(joined(at), joined(after(at, rows)))
        left[at, :] = near.astype(left.dtype)
        right[at, :] = away.astype(right.dtype)


def finish_kernel(width, mine, one, two, three, scales, inv_own, own_scale, hidden, out):
    tok = hidden.shape[0]
    grad = (mine[...] + wide(one[...])) + (wide(two[...]) + wide(three[...]))
    grad = (grad * scales[0:1, :] * own_scale[...]).T
    grad = jnp.concatenate([grad[:tok], grad[tok:]], axis=1)
    columns = jnp.concatenate([scales[1:2, :], inv_own[...], jnp.zeros((6, LANES), jnp.float32)], axis=0).T
    dot, inv = columns[:tok, 0:1], columns[:tok, 1:2]
    out[...] = inv * grad - wide(hidden[...]) * (dot * inv * inv / width)


def call(kernel, name, outs, in_specs, out_specs, scratch, limit, flops, moved, *args):
    return pl.pallas_call(
        kernel,
        out_shape=outs,
        in_specs=in_specs,
        out_specs=out_specs,
        scratch_shapes=scratch,
        compiler_params=pltpu.CompilerParams(vmem_limit_bytes=limit << 20),
        cost_estimate=pl.CostEstimate(flops=flops, bytes_accessed=moved, transcendentals=0),
        name=name,
    )(*args)


def fast_path(hidden, norm_gain, weight, targets, segment_ids, pairing, ref_logp):
    n_sec = lax.axis_size("section")
    n_dp = lax.axis_size("dp")
    n_z = n_sec // 2
    tok, cols = hidden.shape
    tokens = n_dp * tok
    width = cols * n_sec
    vocab = weight.shape[0]
    block = 2 * cols
    padded = -(-vocab // LANES) * LANES
    shape = jax.ShapeDtypeStruct
    half, full = jnp.bfloat16, jnp.float32

    def pairs(of):
        return [(s * n_dp + d, of(s, d)) for s in range(n_sec) for d in range(n_dp)]

    both_axes = ("section", "dp")
    one_pairs = pairs(lambda s, d: (s ^ 1) * n_dp + d if d & 1 == 0 else s * n_dp + (d ^ 2))
    two_pairs = pairs(lambda s, d: (s ^ 1) * n_dp + d if d & 1 == 1 else s * n_dp + (d ^ 2))
    to_one = lambda a: lax.ppermute(a, both_axes, one_pairs)
    to_two = lambda a: lax.ppermute(a, both_axes, two_pairs)
    over_core = lambda a: exchange(a, "dp", n_dp, 1)
    over_x = lambda a: exchange(a, "section", n_sec, 1)
    over_y = lambda a: exchange(a, "dp", n_dp, 2)
    over_z = lambda a, k: exchange(a, "section", n_sec, 2 * k)

    def hold(value, *others):
        return lax.optimization_barrier((value,) + others)[0]

    strips = [hidden] + [over_z(hidden, k) for k in range(1, n_z)]

    strips[0], flat = call(
        functools.partial(own_strip_kernel, vocab), "own_strip",
        (shape((cols // 2, LANES), half), shape((1, tokens), jnp.int32)),
        [VMEM, VMEM], (VMEM, VMEM), [], 4, 0, 16 * width * LANES, hidden, targets,
    )
    base = call(
        strips_kernel, "strips", shape((n_z * cols // 2, LANES), half), [VMEM] * n_z, VMEM, [], 4,
        tok * width, 0, *strips,
    )
    turned_a, turned_b, hit_keep, hit_send = call(
        functools.partial(turn_kernel, cols, n_z), "turn_weight",
        (shape((width // 2, vocab), half),) * 2
        + (shape((width, LANES), half),) * 2,
        [VMEM, VMEM], (VMEM,) * 4, [pltpu.VMEM((vocab, tokens), half)],
        8, 2 * tokens * vocab * width, 4 * vocab * width, hold(flat, base), weight,
    )

    one = to_one(base)
    two = to_two(base)
    table = call(
        gain_kernel, "gain_table", shape((width, LANES), full), [VMEM], VMEM, [], 4, width * LANES,
        16 * width * LANES, hold(norm_gain.reshape(-1, LANES), base),
    )
    half_rows = (shape((width // 2, LANES), half),) * 2
    hit_keep, hit_send = call(
        fold_core_kernel, "fold_rows", half_rows, [VMEM, VMEM], (VMEM, VMEM), [], 4,
        0, 96 * width * LANES, hit_keep, over_core(hold(hit_send, one, two)),
    )
    three = to_two(one)
    stacks = [base, one, two, three]
    stacks = stacks + [over_core(s) for s in (base, one, two, hold(three, hit_send, table))]
    hit_got = to_one(hold(hit_send, three, table))

    normed, inv_own, own_scale = call(
        functools.partial(norm_kernel, cols, n_z), "norm",
        (shape((width, tokens), half), shape((1, LANES), full), shape((cols // 2, LANES), full)),
        [VMEM] * 9, (VMEM,) * 3, [], 4, 8 * tokens * width, 0, *stacks, table,
    )
    raw_logits = lax.dot_general(
        weight, normed, (((1,), (0,)), ((), ())), preferred_element_type=jnp.float32
    )
    bent = jnp.tanh(raw_logits / SOFTCAP)
    hot = lax.broadcasted_iota(jnp.int32, (vocab, 1), 0) == flat
    power = jnp.where(hot, 0.0, jnp.exp(SOFTCAP * bent))
    sloped = power * (1.0 - bent * bent)
    stats = [
        jnp.sum(power, axis=0),
        jnp.sum(sloped * raw_logits, axis=0),
        jnp.sum(jnp.where(hot, raw_logits, 0.0), axis=0),
    ]
    stats = jnp.stack(stats)
    sloped = hold(sloped.astype(half), stats)

    def product(turned, sloped):
        return lax.dot_general(turned, sloped, (((1,), (0,)), ((), ())), preferred_element_type=full)

    def halved(kind, rows):
        return (shape((rows, LANES), kind), shape((rows, LANES), half))

    def fold(kernel, name, mine, got, kind=full):
        return call(
            kernel, name, halved(kind, mine.shape[0] // 2), [VMEM] * 2, (VMEM,) * 2, [], 4, 0, 0, mine, got
        )

    rows = width // 2
    grad_a = product(turned_a, sloped)
    send_a = call(post_kernel, "post", shape((rows, LANES), half), [VMEM], VMEM, [], 4, 0, 0, grad_a)
    got_a = over_core(send_a)
    sums = call(
        count_kernel, "count", shape((8, LANES), full), [VMEM] * 2, VMEM, [], 4, 0, 0, stats, over_core(stats)
    )
    grad_b = product(turned_b, hold(sloped, send_a, sums))
    sums = sums + over_x(sums)
    send_b = call(post_kernel, "post", shape((rows, LANES), half), [VMEM], VMEM, [], 4, 0, 0, hold(grad_b, sums))
    got_b = over_core(hold(send_b, hit_got))
    keep_a, send_a = fold(fold_core_kernel, "fold_core", grad_a, hold(got_a, sums))
    got_a = to_one(send_a)
    heard = over_y(sums)
    keep_b, send_b = fold(fold_core_kernel, "fold_core", grad_b, hold(got_b, send_a))
    got_b = to_one(send_b)
    sums = sums + jnp.concatenate([heard[:, HALF:], heard[:, :HALF]], axis=1)
    sums = sums + over_z(sums, 1)
    heard = over_z(sums, 2)

    rows = width // 4

    def join(name, first_row, mine, got):
        return call(
            functools.partial(join_kernel, first_row), name, halved(full, rows // 2),
            [VMEM] * 6, (VMEM,) * 2, [], 4, 0, 0, mine, got, hit_keep, hit_got, sums, heard,
        )

    keep_a, send_a = join("join_a", 0, keep_a, got_a)
    got_a = to_two(send_a)
    keep_b, send_b = join("join_b", rows, keep_b, hold(got_b, send_a))
    got_b = to_two(send_b)
    send_1, send_3 = fold(fold_half_kernel, "fold_last_a", keep_a, got_a, half)
    got_3, got_1 = over_z(send_3, 3), over_z(send_1, 1)
    keep, send_2 = fold(fold_half_kernel, "fold_last_b", keep_b, hold(got_b, send_3))
    got_2 = over_z(send_2, 2)
    scales, margins, dpo_loss = call(
        tally_kernel, "tally",
        (shape((8, LANES), full), shape((1, ref_logp.shape[1] // 2), full), shape((1, 1), full)),
        [VMEM] * 5, (VMEM,) * 3, [], 4, 0, 0, sums, hold(heard, send_2), segment_ids, pairing, ref_logp,
    )
    hidden_grad = call(
        functools.partial(finish_kernel, width), "finish", shape((tok, cols), full),
        [VMEM] * 8, VMEM, [], 4, 0, 0,
        keep, got_1, got_2, got_3, scales, inv_own, own_scale, hidden,
    )
    return (hidden_grad, margins, dpo_loss.reshape(()))


def per_device(hidden, norm_gain, weight, *rest):
    n_sec, n_dp = lax.axis_size("section"), lax.axis_size("dp")
    tok, cols = hidden.shape
    vocab = weight.shape[0]
    fits = n_dp == 4 and n_sec == 8 and tok == HALF and cols % HALF == 0 and vocab % 8 == 0
    fits = fits and norm_gain.shape[0] % LANES == 0
    path = fast_path if fits else general_path
    return path(hidden, norm_gain, weight, *rest)


def solution(mesh):
    in_specs = (P("dp", "section"), P(), P(("section", "dp"), None), P(), P(), P(), P())
    out_specs = (P("dp", "section"), P("dp", None), P())
    return jax.shard_map(
        per_device, mesh=mesh, in_specs=in_specs, out_specs=out_specs, check_vma=False
    )
```
